256 devices in a mesh: ta: 4 (over y), xyz: 64 (over z, x, core).
Axes of the slice: x: 4, y: 4, z: 8, core: 2. Of those that a mesh axis runs over, the one named last changes fastest.
Arguments:
- vectors: bfloat16 [8, 3, 32768, 128], P('ta', None, 'xyz'), parts along dimension 0, may hold values from -6 to 6
- links: bfloat16 [12, 2, 3, 3, 32768], P('ta', None, None, None, 'xyz'), parts along dimension 0, may hold values from -2.5 to 2.5
- momenta: int32 [2, 3], replicated, may hold values from -2 to 2
- directions: int32 [3], replicated, may hold values from 0 to 2, each once
Outputs:
- elementals: float32 [8, 3, 2, 128, 128], P('ta', None, None, 'xyz'), parts along dimension 0
The draws below stay inside these ranges and needn't reach their ends.
There are 4 independent parts, one for each index of `ta`. The reference program is written for one: setup_inputs(seed, part) draws one part's arguments, and reference() takes and returns one part's arrays. A program takes and returns all parts, laid end to end along the dimension named above; an argument that names none is the same for every part. Nothing has to cross between parts.
Inputs may be any that keep to these rules, and one draw needn't show every extreme that they name: `directions`: each lattice direction appears once.
All inputs are finite; a program needn't handle non-finite values.
Results may differ from the reference program's by a relative error of at most 0.0039.
Values may be sent and summed in bfloat16 or wider, within the bound.
No kernel may reach another device: no remote copies, remote signals or barrier semaphores. Data moves between devices by JAX's collectives and lax.ppermute only.
A program may use at most 64 MiB of HBM per device.

```python
import math
import jax
import jax.numpy as jnp
from jax import lax

SIDE = 8
NVEC = 128
NMOM = 2
GRID = 4
LSIDE = 32
SITES = 32768


def with_ends(array, key, smallest, largest):
    index_at = [jax.random.randint(jax.random.fold_in(key, axis), (), 0, length) for axis, length in enumerate(array.shape)]
    main_axis = array.shape.index(max(array.shape))
    neighbour = index_at[:main_axis] + [(index_at[main_axis] + 1) % array.shape[main_axis]] + index_at[main_axis + 1:]
    return array.at[tuple(index_at)].set(smallest).at[tuple(neighbour)].set(largest)


def block_scale(key, extent, split, least, largest):
    def one(dim, blocks):
        heights = jax.random.uniform(jax.random.fold_in(jax.random.fold_in(key, 6), dim), (blocks,), jnp.float32, least / len(split), largest / len(split))
        return jnp.repeat(jnp.exp(heights), extent[dim] // blocks).reshape((-1,) + (1,) * (len(extent) - dim - 1))

    level = one(*split[0])
    for cut in split[1:]:
        level = level * one(*cut)
    return level


def gaussian(key, dims, scale, limit, cuts=(), held_as=jnp.bfloat16):
    factor_of = block_scale(key, dims, cuts, -0.22, 0.18) if cuts else 1.0
    entries = jax.random.normal(key, dims, jnp.float32) * scale * factor_of
    return jnp.minimum(jnp.maximum(entries, -limit), limit).astype(held_as)


def setup_inputs(seed: int = 0, part: int = 0) -> dict:
    arg_keys = jax.random.split(jax.random.key(seed), 5)
    part_splits = jax.random.split(jax.random.fold_in(arg_keys[4], part), 5)
    return {
        "vectors": gaussian(part_splits[0], (2, 3, SITES, NVEC), 1.0, 6.0, ((2, 64),)),
        "links": gaussian(part_splits[1], (3, 2, 3, 3, SITES), 6 ** -0.5, 2.5, ((4, 64),)),
        "momenta": with_ends(jax.random.randint(arg_keys[2], (NMOM, 3), -2, 3), jax.random.fold_in(arg_keys[2], 1), -2, 2).astype(jnp.int32),
        "directions": jax.random.permutation(arg_keys[3], 3).astype(jnp.int32),
    }


def to_lattice(flat_field, leading):
    shape_lead = flat_field.shape[:leading]
    trailing = flat_field.shape[leading + 1:]
    pieces = flat_field.reshape(shape_lead + (GRID, GRID, GRID, SIDE, SIDE, SIDE) + trailing)
    pieces = jnp.flip(pieces, axis=leading + 1)
    axis_order = list(range(leading)) + [leading, leading + 3, leading + 1, leading + 4, leading + 2, leading + 5] + list(range(leading + 6, pieces.ndim))
    return jnp.transpose(pieces, axis_order).reshape(shape_lead + (LSIDE, LSIDE, LSIDE) + trailing)

def reference(vectors, links, momenta, directions):
    lattice_vectors = to_lattice(vectors, 2)
    lattice_links = to_lattice(links, 4)
    coords = jnp.arange(LSIDE, dtype=jnp.int32)
    phase_index = (momenta[:, 0, None, None, None] * coords[None, :, None, None] + momenta[:, 1, None, None, None] * coords[None, None, :, None] + momenta[:, 2, None, None, None] * coords[None, None, None, :]) % LSIDE
    angles = phase_index.astype(jnp.float32) * (2.0 * math.pi / LSIDE)
    cosine = jnp.moveaxis(jnp.cos(angles), 0, -1)[None, :, :, :, :, None]
    sine_part = jnp.moveaxis(jnp.sin(angles), 0, -1)[None, :, :, :, :, None]
    real_vec = lattice_vectors[0].astype(jnp.float32)[:, :, :, :, None, :]
    imag_vec = lattice_vectors[1].astype(jnp.float32)[:, :, :, :, None, :]
    left_factor = jnp.stack([cosine * real_vec - sine_part * imag_vec, sine_part * real_vec + cosine * imag_vec]).astype(jnp.bfloat16)
    left_matrix = left_factor.astype(jnp.float32).reshape(6 * LSIDE ** 3, NMOM * NVEC)
    results = []
    for lattice_dim in range(3):
        shifted = jnp.roll(lattice_vectors, -1, axis=2 + lattice_dim).astype(jnp.float32).reshape(6, LSIDE ** 3, NVEC)
        link_pair = lattice_links[lattice_dim].astype(jnp.float32).reshape(2, 3, 3, LSIDE ** 3)
        real_form = jnp.concatenate([jnp.concatenate([link_pair[0], -link_pair[1]], axis=1), jnp.concatenate([link_pair[1], link_pair[0]], axis=1)], axis=0)
        product = jnp.einsum('ijs,jsn->isn', real_form, shifted, precision=lax.Precision.HIGHEST).astype(jnp.bfloat16)
        swapped = jnp.concatenate([product[3:], -product[:3]], axis=0)
        right_matrix = jnp.stack([product, swapped], axis=2).astype(jnp.float32).reshape(6 * LSIDE ** 3, 2 * NVEC)
        summed = jnp.dot(left_matrix.T, right_matrix, precision=lax.Precision.HIGHEST, preferred_element_type=jnp.float32)
        results.append(summed.reshape(NMOM, NVEC, 2, NVEC))
    elemental_set = jnp.stack(results)
    chosen = elemental_set[directions]
    return jnp.transpose(chosen, (3, 0, 1, 2, 4)) * (1.0 / math.sqrt(3.0 * SITES))
```

```python
import functools
import math

import jax
import jax.numpy as jnp
from jax import lax
from jax.experimental import pallas as pl
from jax.experimental.pallas import tpu as pltpu
from jax.sharding import PartitionSpec as P

SIDE = 8
SITES = 512
FACE = 64
NVEC = 128
F32 = jnp.float32
BF16 = jnp.bfloat16
VMEM = pl.BlockSpec(memory_space=pltpu.VMEM)
SMEM = pl.BlockSpec(memory_space=pltpu.SMEM)
NT = (((1,), (1,)), ((), ()))


def face_site(face, direction, last):
    hi, lo = face >> 3, face & 7
    edge = SIDE - 1 if last else 0
    if direction == 0:
        return edge * 64 + face
    if direction == 1:
        return hi * 64 + edge * 8 + lo
    return face * 8 + edge


def layer_kernel(v_ref, x_ref, y_ref, z_ref):
    site = lax.broadcasted_iota(jnp.int32, (FACE, SITES), 1)
    face = lax.broadcasted_iota(jnp.int32, (FACE, SITES), 0)
    picks = [(site == face_site(face, d, False)).astype(BF16) for d in range(3)]
    pick = jnp.concatenate(picks, axis=0)
    for rc in range(6):
        layers = jnp.dot(pick, v_ref[rc], preferred_element_type=F32).astype(BF16)
        x_ref[rc] = layers[0:64]
        y_ref[rc] = layers[64:128]
        z_ref[rc] = layers[128:192]


def interior_kernel(mom_ref, v_ref, u_ref, part_ref, lf_ref, uf_ref, vt, lt, rt, ub, us):
    index = lax.axis_index("xyz")
    gx, gy, gz = index // 16, 3 - (index // 4) % 4, index % 4
    eye = (
        lax.broadcasted_iota(jnp.int32, (NVEC, NVEC), 0)
        == lax.broadcasted_iota(jnp.int32, (NVEC, NVEC), 1)
    ).astype(BF16)
    for rc in range(6):
        vt[rc] = lax.dot_general(eye, v_ref[rc], NT, preferred_element_type=F32)

    site = lax.broadcasted_iota(jnp.int32, (8, SITES), 1)
    lx, ly, lz = site >> 6, (site >> 3) & 7, site & 7
    phases = []
    for p in range(2):
        k = (
            mom_ref[p, 0] * (gx * 8 + lx)
            + mom_ref[p, 1] * (gy * 8 + ly)
            + mom_ref[p, 2] * (gz * 8 + lz)
        ) & 31
        angle = k.astype(F32) * (2.0 * math.pi / 32)
        phases.append((jnp.cos(angle)[None], jnp.sin(angle)[None]))

    inner = [(local < SIDE - 1).astype(F32) for local in (lx, ly, lz)]
    for d in range(3):
        for ij in range(9):
            pair = u_ref[d * 9 + ij].astype(F32)
            us[pl.ds((d * 9 + ij) * 2, 2), :] = pair
            for r in range(2):
                ub[d * 18 + ij * 2 + r] = pair[r : r + 1] * inner[d]
    us[pl.ds(54, 10), :] = jnp.zeros((10, SITES), F32)

    upper = lax.broadcasted_iota(jnp.int32, (1, 8, 128), 2) >= 64

    def rows_step(block, _):
        row = pl.multiple_of(block * 16, 16)
        rows = pl.ds(row, 16)
        for c in range(3):
            re = vt[c, rows, :].reshape(2, 8, SITES)
            im = vt[3 + c, rows, :].reshape(2, 8, SITES)
            for p in range(2):
                cosine, sine = phases[p]
                lanes = pl.ds(c * SITES, SITES)
                out = pl.ds(pl.multiple_of(p * 128 + row, 16), 16)
                lt[out, lanes] = (cosine * re - sine * im).reshape(16, SITES).astype(BF16)
                out = pl.ds(pl.multiple_of(256 + p * 128 + row, 16), 16)
                lt[out, lanes] = (sine * re + cosine * im).reshape(16, SITES).astype(BF16)
        for d in range(3):
            for k in range(4):
                lanes = pl.ds(k * 128, 128)
                shifted = []
                for rc in range(6):
                    here = vt[rc, rows, lanes]
                    if d == 2:
                        here = pltpu.roll(here, 127, 1)
                    elif d == 1:
                        here = pltpu.roll(here, 120, 1)
                    else:
                        here = pltpu.roll(here, 64, 1)
                        if k < 3:
                            after = pltpu.roll(vt[rc, rows, pl.ds(k * 128 + 128, 128)], 64, 1)
                            here = jnp.where(upper[0, 0:1], after, here)
                    shifted.append(here.reshape(2, 8, 128))
                for i in range(3):
                    dr = di = None
                    for j in range(3):
                        ur = ub[d * 18 + i * 6 + j * 2, :, lanes][None]
                        ui = ub[d * 18 + i * 6 + j * 2 + 1, :, lanes][None]
                        vr, vi = shifted[j], shifted[3 + j]
                        tr, ti = ur * vr - ui * vi, ui * vr + ur * vi
                        dr, di = (tr, ti) if dr is None else (dr + tr, di + ti)
                    lanes_out = pl.ds(i * SITES + k * 128, 128)
                    rt[d, rows, lanes_out] = dr.reshape(16, 128).astype(BF16)
                    out = pl.ds(pl.multiple_of(128 + row, 16), 16)
                    rt[d, out, lanes_out] = di.reshape(16, 128).astype(BF16)
        return 0

    lax.fori_loop(0, 8, rows_step, 0)

    for d in range(3):
        full = lax.dot_general(lt[...], rt[d], NT, preferred_element_type=F32)
        for p in range(2):
            re_rows, im_rows = full[p * 128 : p * 128 + 128], full[256 + p * 128 : 384 + p * 128]
            part_ref[d * 4 + p * 2] = re_rows[:, :128] + im_rows[:, 128:]
            part_ref[d * 4 + p * 2 + 1] = re_rows[:, 128:] - im_rows[:, :128]

    site_c = lax.broadcasted_iota(jnp.int32, (SITES, FACE), 0)
    face_c = lax.broadcasted_iota(jnp.int32, (SITES, FACE), 1)
    site_r = lax.broadcasted_iota(jnp.int32, (FACE, SITES), 1)
    face_r = lax.broadcasted_iota(jnp.int32, (FACE, SITES), 0)
    for d in range(3):
        pick_c = (site_c == face_site(face_c, d, True)).astype(BF16)
        pick_r = (site_r == face_site(face_r, d, True)).astype(BF16)
        for c in range(3):
            lf_ref[d, c] = jnp.dot(
                lt[:, c * SITES : (c + 1) * SITES], pick_c, preferred_element_type=F32
            ).astype(BF16)
        uf_ref[d] = lax.dot_general(pick_r, us[...].astype(BF16), NT, preferred_element_type=F32)


def boundary_kernel(part_ref, lf_ref, uf_ref, x_ref, y_ref, z_ref, send_ref, keep_ref, tile, chunk):
    core = lax.axis_index("xyz") % 2
    for d, layer_ref in enumerate((x_ref, y_ref, z_ref)):
        total = None
        layer = [layer_ref[rc].astype(F32) for rc in range(6)]
        for i in range(3):
            dr = di = None
            for j in range(3):
                q = d * 18 + i * 6 + j * 2
                ur = jnp.broadcast_to(uf_ref[d, :, q : q + 1], (FACE, NVEC))
                ui = jnp.broadcast_to(uf_ref[d, :, q + 1 : q + 2], (FACE, NVEC))
                vr, vi = layer[j], layer[3 + j]
                tr, ti = ur * vr - ui * vi, ui * vr + ur * vi
                dr, di = (tr, ti) if dr is None else (dr + tr, di + ti)
            right = jnp.concatenate([dr.astype(BF16), di.astype(BF16)], axis=1)
            term = jnp.dot(lf_ref[d, i], right, preferred_element_type=F32)
            total = term if total is None else total + term
        for p in range(2):
            re_rows, im_rows = total[p * 128 : p * 128 + 128], total[256 + p * 128 : 384 + p * 128]
            t = d * 4 + p * 2
            tile[t] = part_ref[t] + re_rows[:, :128] + im_rows[:, 128:]
            tile[t + 1] = part_ref[t + 1] + re_rows[:, 128:] - im_rows[:, :128]
    for which, parity in ((0, core), (1, 1 - core)):
        for t in range(12):
            for r in range(2):
                rows = tile[t, pl.ds(2 * parity + r, 32, stride=4), :]
                chunk[which, pl.ds(t * 2 + r, 32, stride=24), :] = rows
    keep_ref[...] = chunk[0]
    send_ref[...] = chunk[1].astype(BF16)


def final_kernel(scale, dir_ref, got_ref, out_ref, acc):
    acc[...] = jnp.sum(got_ref[...].astype(F32), axis=0) * scale
    for d in range(3):
        rows = acc[pl.ds(pl.multiple_of(dir_ref[d] * 8, 8), 8), :]
        for p in range(2):
            for o in range(2):
                t = (p * 2 + o) * 2
                out_ref[o, d, p] = rows[t : t + 2]


def shape(dims, dtype):
    return jax.ShapeDtypeStruct(dims, dtype)


def per_device(vectors, links, momenta, directions):
    params = pltpu.CompilerParams(vmem_limit_bytes=48 * 1024 * 1024)
    field = vectors.reshape(6, SITES, NVEC)
    rows = links.transpose(0, 2, 3, 1, 4).reshape(27, 2, SITES)
    face = shape((6, FACE, NVEC), BF16)
    layers = pl.pallas_call(
        layer_kernel,
        out_shape=[face] * 3,
        in_specs=[VMEM],
        out_specs=[VMEM] * 3,
        compiler_params=params,
    )(field)
    step_x = [(i, (i - 16) % 64) for i in range(64)]
    step_y = [(i, (i & ~12) | ((i + 4) & 12)) for i in range(64)]
    step_z = [(i, (i & ~3) | ((i - 1) & 3)) for i in range(64)]
    arrived = [lax.ppermute(a, "xyz", s) for a, s in zip(layers, (step_x, step_y, step_z))]
    part, left_face, link_face = pl.pallas_call(
        interior_kernel,
        out_shape=[
            shape((12, NVEC, NVEC), F32),
            shape((3, 3, 512, FACE), BF16),
            shape((3, FACE, 64), F32),
        ],
        in_specs=[SMEM, VMEM, VMEM],
        out_specs=[VMEM] * 3,
        scratch_shapes=[
            pltpu.VMEM((6, NVEC, SITES), F32),
            pltpu.VMEM((512, 3 * SITES), BF16),
            pltpu.VMEM((3, 256, 3 * SITES), BF16),
            pltpu.VMEM((54, 8, SITES), F32),
            pltpu.VMEM((64, SITES), F32),
        ],
        compiler_params=params,
        cost_estimate=pl.CostEstimate(
            flops=2_000_000_000, bytes_accessed=4_000_000, transcendentals=0
        ),
    )(momenta, field, rows)
    send, keep = pl.pallas_call(
        boundary_kernel,
        out_shape=[shape((768, NVEC), BF16), shape((768, NVEC), F32)],
        in_specs=[VMEM] * 6,
        out_specs=[VMEM] * 2,
        scratch_shapes=[pltpu.VMEM((12, NVEC, NVEC), F32), pltpu.VMEM((2, 768, NVEC), F32)],
        compiler_params=params,
    )(part, left_face, link_face, *arrived)
    other = lax.ppermute(send, "xyz", [(i, i ^ 1) for i in range(64)])
    chip = (keep + other.astype(F32)).astype(BF16).reshape(32, 24, NVEC)
    groups = [[2 * c + core for c in range(32)] for core in range(2)]
    got = lax.all_to_all(chip, "xyz", 0, 0, axis_index_groups=groups, tiled=True)
    return pl.pallas_call(
        functools.partial(final_kernel, 1.0 / math.sqrt(3.0 * SITES * 64)),
        out_shape=shape((2, 3, 2, 2, NVEC), F32),
        in_specs=[SMEM, VMEM],
        out_specs=VMEM,
        scratch_shapes=[pltpu.VMEM((24, NVEC), F32)],
        compiler_params=params,
    )(directions, got)


def solution(mesh):
    in_specs = (P("ta", None, "xyz", None), P("ta", None, None, None, "xyz"), P(), P())
    out_specs = P("ta", None, None, "xyz", None)
    return jax.shard_map(
        per_device, mesh=mesh, in_specs=in_specs, out_specs=out_specs, check_vma=False
    )
```

```python
import functools
import math

import jax
import jax.numpy as jnp
from jax import lax
from jax.experimental import pallas as pl
from jax.experimental.pallas import tpu as pltpu
from jax.sharding import PartitionSpec as P

SIDE = 8
SITES = 512
FACE = 64
NVEC = 128
F32 = jnp.float32
BF16 = jnp.bfloat16
VMEM = pl.BlockSpec(memory_space=pltpu.VMEM)
HBM = pl.BlockSpec(memory_space=pltpu.HBM)
NT = (((1,), (1,)), ((), ()))


def iota(dims, axis):
    return lax.broadcasted_iota(jnp.int32, dims, axis)


def face_site(face, direction):
    hi, lo = face >> 3, face & 7
    return ((SIDE - 1) * 64 + face, hi * 64 + (SIDE - 1) * 8 + lo, face * 8 + SIDE - 1)[direction]


def layers(ref, index, layer):
    yield ref[index, pl.ds(layer * 64, 64), :]
    yield jnp.concatenate([ref[index, pl.ds(n * 64 + layer * 8, 8), :] for n in range(8)], axis=0)
    yield ref[index, pl.ds(layer, 64, stride=8), :]


def layer_kernel(v_ref, held_ref, x_ref, y_ref, z_ref, wide):
    for rc in range(6):
        wide[rc] = v_ref[rc].astype(F32)
        for out_ref, rows in zip((x_ref, y_ref, z_ref), layers(wide, rc, 0)):
            out_ref[rc] = rows.astype(BF16)


def link_product(link, shifted):
    for i in range(3):
        dr = di = None
        for j in range(3):
            ur, ui = link(i, j)
            vr, vi = shifted[j], shifted[3 + j]
            tr, ti = ur * vr - ui * vi, ui * vr + ur * vi
            dr, di = (tr, ti) if dr is None else (dr + tr, di + ti)
        yield i, dr, di


def complex_parts(full):
    top, bottom = full[:128], full[128:]
    return top[:, :128] + bottom[:, 128:], top[:, 128:] - bottom[:, :128]


def interior_kernel(
    mom_hbm, u, v_ref, part0_ref, part1_ref, lf0_ref, lf1_ref, uf_ref,
    mom, sem, wide, vt, vo, vl, lt, rt, ub, us, ut,
):
    copy = pltpu.make_async_copy(mom_hbm, mom, sem)
    copy.start()
    index = lax.axis_index("xyz")
    gx, gy, gz, core = index // 16, 3 - (index // 4) % 4, index % 4, index % 2

    row, column = iota((256, NVEC), 0), iota((256, NVEC), 1)
    whose = jnp.where(row < 128, 1 - core, core)
    order = (column == 4 * ((row >> 2) & 31) + 2 * whose + (row & 1)).astype(BF16)
    plain = (iota((NVEC, NVEC), 0) == iota((NVEC, NVEC), 1)).astype(BF16)
    both = jnp.concatenate([plain, order], axis=0)
    for rc in range(6):
        turned = lax.dot_general(both, v_ref[rc], NT, preferred_element_type=F32)
        for k in range(4):
            vt[rc, k] = turned[:128, k * 128 : k * 128 + 128]
        vo[rc] = turned[128:]
        wide[rc] = v_ref[rc].astype(F32)
        last = jnp.concatenate(list(layers(wide, rc, SIDE - 1)), axis=0).astype(BF16)
        turned = lax.dot_general(order, last, NT, preferred_element_type=F32)
        for d in range(3):
            place = pl.ds((rc % 3) * FACE, FACE)
            vl[d * 2 + rc // 3, :, place] = turned[:, d * FACE : d * FACE + FACE]
    copy.wait()

    def phase(site):
        lx, ly, lz = site >> 6, (site >> 3) & 7, site & 7
        second = ((iota(site.shape, 0) >> 1) & 1) == 1
        m = [jnp.where(second, mom[1, axis], mom[0, axis]) for axis in range(3)]
        k = (m[0] * (gx * 8 + lx) + m[1] * (gy * 8 + ly) + m[2] * (gz * 8 + lz)) & 31
        angle = k.astype(F32) * (2.0 * math.pi / 32)
        return jnp.cos(angle)[None], jnp.sin(angle)[None]

    def rotate(re, im, turn, width):
        cosine, sine = turn
        re, im = re.reshape(-1, 8, width), im.reshape(-1, 8, width)
        left = (cosine * re - sine * im).reshape(-1, width).astype(BF16)
        return left, (sine * re + cosine * im).reshape(-1, width).astype(BF16)

    site = iota((8, SITES), 1)
    turn = phase(site)
    for block in range(16):
        rows = pl.ds(block * 16, 16)
        for c in range(3):
            left = rotate(vo[c, rows, :], vo[3 + c, rows, :], turn, SITES)
            for ri in range(2):
                out = pl.ds((block // 8) * 256 + ri * 128 + (block % 8) * 16, 16)
                lt[out, pl.ds(c * SITES, SITES)] = left[ri]
    for d in range(3):
        turn = phase(face_site(iota((8, 3 * FACE), 1) & 63, d))
        left = rotate(vl[d * 2], vl[d * 2 + 1], turn, 3 * FACE)
        for ri in range(2):
            lf0_ref[d, pl.ds(ri * 128, 128), :] = left[ri][:128]
            lf1_ref[d, pl.ds(ri * 128, 128), :] = left[ri][128:]

    inner = [(n < SIDE - 1).astype(F32) for n in (site >> 6, (site >> 3) & 7, site & 7)]
    us[pl.ds(54, 74), :] = jnp.zeros((74, SITES), F32)
    for d in range(3):
        for ij in range(9):
            pair = u[d * 9 + ij].astype(F32)
            us[pl.ds((d * 9 + ij) * 2, 2), :] = pair
            for r in range(2):
                ub[d * 18 + ij * 2 + r] = pair[r : r + 1] * inner[d]
    for k in range(4):
        ut[0, pl.ds(k * 128, 128), :] = us[:, k * 128 : k * 128 + 128].T
    for d, rows in enumerate(layers(ut, 0, SIDE - 1)):
        uf_ref[d] = rows

    upper = iota((16, 128), 1) >= 64
    for d in range(3):
        for block in range(8):
            rows = pl.ds(block * 16, 16)
            for k in range(4):
                lanes = pl.ds(k * 128, 128)
                shifted = []
                for rc in range(6):
                    here = pltpu.roll(vt[rc, k, rows, :], (64, 120, 127)[d], 1)
                    if d == 0 and k < 3:
                        after = pltpu.roll(vt[rc, k + 1, rows, :], 64, 1)
                        here = jnp.where(upper, after, here)
                    shifted.append(here.reshape(2, 8, 128))

                def link(i, j):
                    q = d * 18 + i * 6 + j * 2
                    return ub[q, :, lanes][None], ub[q + 1, :, lanes][None]

                for i, dr, di in link_product(link, shifted):
                    lanes_out = pl.ds(i * SITES + k * 128, 128)
                    rt[d, rows, lanes_out] = dr.reshape(16, 128).astype(BF16)
                    rt[d, pl.ds(128 + block * 16, 16), lanes_out] = di.reshape(16, 128).astype(BF16)
    for d in range(3):
        full = lax.dot_general(lt[...], rt[d], NT, preferred_element_type=F32)
        for half, out_ref in enumerate((part0_ref, part1_ref)):
            re, im = complex_parts(full[half * 256 : half * 256 + 256])
            out_ref[d * 2] = re
            out_ref[d * 2 + 1] = im


def boundary_half(part_ref, lf_ref, right, chunk):
    low = iota((16, 8, NVEC), 1) < 4
    for d in range(3):
        term = jnp.dot(lf_ref[d], right(d), preferred_element_type=F32)
        re, im = complex_parts(term)
        re = (part_ref[d * 2] + re).reshape(16, 8, NVEC)
        im = (part_ref[d * 2 + 1] + im).reshape(16, 8, NVEC)
        even = jnp.where(low, re, pltpu.roll(im, 4, 1))
        odd = jnp.where(low, pltpu.roll(re, 4, 1), im)
        pairs = jnp.stack([even, odd], axis=1).reshape(32, 8, NVEC)
        chunk[:, pl.ds(d * 8, 8), :] = pairs


def send_kernel(part_ref, lf_ref, uf_ref, x_ref, y_ref, z_ref, send_ref, right_ref, chunk):
    for d, layer_ref in enumerate((x_ref, y_ref, z_ref)):
        layer = [layer_ref[rc].astype(F32) for rc in range(6)]

        def link(i, j):
            q = d * 18 + i * 6 + j * 2
            return (
                jnp.broadcast_to(uf_ref[d, :, q : q + 1], (FACE, NVEC)),
                jnp.broadcast_to(uf_ref[d, :, q + 1 : q + 2], (FACE, NVEC)),
            )

        for i, dr, di in link_product(link, layer):
            right_ref[d, pl.ds(i * FACE, FACE), pl.ds(0, NVEC)] = dr.astype(BF16)
            right_ref[d, pl.ds(i * FACE, FACE), pl.ds(NVEC, NVEC)] = di.astype(BF16)
    boundary_half(part_ref, lf_ref, lambda d: right_ref[d], chunk)
    send_ref[...] = chunk[...].reshape(768, NVEC).astype(BF16)


def keep_kernel(dir_hbm, part_ref, lf_ref, right_ref, keep_ref, asked_ref, dirs, sem, chunk):
    copy = pltpu.make_async_copy(dir_hbm, dirs, sem)
    copy.start()
    boundary_half(part_ref, lf_ref, lambda d: right_ref[d], chunk)
    keep_ref[...] = chunk[...].reshape(768, NVEC)
    copy.wait()
    for slot in range(3):
        asked_ref[slot] = jnp.full((8, NVEC), dirs[slot], jnp.int32)


def final_kernel(scale, asked_ref, got_ref, out_ref):
    rows = jnp.sum(got_ref[...].astype(F32), axis=0) * scale
    for slot in range(3):
        chosen = jnp.where(asked_ref[slot] == 1, rows[8:16], rows[0:8])
        chosen = jnp.where(asked_ref[slot] == 2, rows[16:24], chosen)
        for o in range(2):
            for p in range(2):
                t = o * 4 + p * 2
                out_ref[o, slot, p] = chosen[t : t + 2]


def shape(dims, dtype):
    return jax.ShapeDtypeStruct(dims, dtype)


def per_device(vectors, links, momenta, directions):
    params = pltpu.CompilerParams(vmem_limit_bytes=48 * 1024 * 1024)
    field = vectors.reshape(6, SITES, NVEC)
    rows = links.transpose(0, 2, 3, 1, 4).reshape(27, 2, SITES)
    face = shape((6, FACE, NVEC), BF16)
    held, *first = pl.pallas_call(
        layer_kernel,
        out_shape=[shape((6, SITES, NVEC), BF16)] + [face] * 3,
        in_specs=[VMEM],
        out_specs=[VMEM] * 4,
        scratch_shapes=[pltpu.VMEM((6, SITES, NVEC), F32)],
        input_output_aliases={0: 0},
        compiler_params=params,
    )(field)
    step_x = [(i, (i - 16) % 64) for i in range(64)]
    step_y = [(i, (i & ~12) | ((i + 4) & 12)) for i in range(64)]
    step_z = [(i, (i & ~3) | ((i - 1) & 3)) for i in range(64)]
    arrived = [lax.ppermute(a, "xyz", s) for a, s in zip(first, (step_x, step_y, step_z))]
    part = shape((6, NVEC, NVEC), F32)
    left = shape((3, 256, 3 * FACE), BF16)
    part0, part1, left0, left1, link_face = pl.pallas_call(
        interior_kernel,
        out_shape=[part, part, left, left, shape((3, FACE, NVEC), F32)],
        in_specs=[HBM] + [VMEM] * 2,
        out_specs=[VMEM] * 5,
        scratch_shapes=[
            pltpu.SMEM((2, 3), jnp.int32),
            pltpu.SemaphoreType.DMA,
            pltpu.VMEM((6, SITES, NVEC), F32),
            pltpu.VMEM((6, 4, NVEC, 128), F32),
            pltpu.VMEM((6, 256, SITES), F32),
            pltpu.VMEM((6, 256, 3 * FACE), F32),
            pltpu.VMEM((512, 3 * SITES), BF16),
            pltpu.VMEM((3, 256, 3 * SITES), BF16),
            pltpu.VMEM((54, 8, SITES), F32),
            pltpu.VMEM((128, SITES), F32),
            pltpu.VMEM((1, SITES, 128), F32),
        ],
        compiler_params=params,
        cost_estimate=pl.CostEstimate(
            flops=2_000_000_000, bytes_accessed=4_000_000, transcendentals=0
        ),
    )(pltpu.with_memory_space_constraint(momenta, pltpu.HBM), rows, held)
    send, right = pl.pallas_call(
        send_kernel,
        out_shape=[shape((768, NVEC), BF16), shape((3, 3 * FACE, 256), BF16)],
        in_specs=[VMEM] * 6,
        out_specs=[VMEM] * 2,
        scratch_shapes=[pltpu.VMEM((32, 24, NVEC), F32)],
        compiler_params=params,
    )(part0, left0, link_face, *arrived)
    other = lax.ppermute(send, "xyz", [(i, i ^ 1) for i in range(64)])
    keep, asked = pl.pallas_call(
        keep_kernel,
        out_shape=[shape((768, NVEC), F32), shape((3, 8, NVEC), jnp.int32)],
        in_specs=[HBM] + [VMEM] * 3,
        out_specs=[VMEM] * 2,
        scratch_shapes=[
            pltpu.SMEM((3,), jnp.int32),
            pltpu.SemaphoreType.DMA,
            pltpu.VMEM((32, 24, NVEC), F32),
        ],
        compiler_params=params,
    )(pltpu.with_memory_space_constraint(directions, pltpu.HBM), part1, left1, right)
    chip = (keep + other.astype(F32)).astype(BF16).reshape(32, 24, NVEC)
    groups = [[2 * c + core for c in range(32)] for core in range(2)]
    got = lax.all_to_all(chip, "xyz", 0, 0, axis_index_groups=groups, tiled=True)
    return pl.pallas_call(
        functools.partial(final_kernel, 1.0 / math.sqrt(3.0 * SITES * 64)),
        out_shape=shape((2, 3, 2, 2, NVEC), F32),
        in_specs=[VMEM] * 2,
        out_specs=VMEM,
        compiler_params=params,
    )(asked, got)


def solution(mesh):
    in_specs = (P("ta", None, "xyz", None), P("ta", None, None, None, "xyz"), P(), P())
    out_specs = P("ta", None, None, "xyz", None)
    return jax.shard_map(
        per_device, mesh=mesh, in_specs=in_specs, out_specs=out_specs, check_vma=False
    )
```

```python
import functools
import math

import jax
import jax.numpy as jnp
from jax import lax
from jax.experimental import pallas as pl
from jax.experimental.pallas import tpu as pltpu
from jax.sharding import PartitionSpec as P

SIDE = 8
SITES = 512
FACE = 64
NVEC = 128
F32 = jnp.float32
BF16 = jnp.bfloat16
VMEM = pl.BlockSpec(memory_space=pltpu.VMEM)
HBM = pl.BlockSpec(memory_space=pltpu.HBM)
NT = (((1,), (1,)), ((), ()))


def iota(dims, axis):
    return lax.broadcasted_iota(jnp.int32, dims, axis)


def face_site(face, direction):
    hi, lo = face >> 3, face & 7
    return ((SIDE - 1) * 64 + face, hi * 64 + (SIDE - 1) * 8 + lo, face * 8 + SIDE - 1)[direction]


def layers(ref, index, layer):
    yield ref[index, pl.ds(layer * 64, 64), :]
    yield jnp.concatenate([ref[index, pl.ds(n * 64 + layer * 8, 8), :] for n in range(8)], axis=0)
    yield ref[index, pl.ds(layer, 64, stride=8), :]


def layer_kernel(v_ref, held_ref, wide, x_ref, y_ref, z_ref):
    for rc in range(6):
        wide[rc] = v_ref[rc].astype(F32)
        for out_ref, rows in zip((x_ref, y_ref, z_ref), layers(wide, rc, 0)):
            out_ref[rc] = rows.astype(BF16)


def link_product(link, shifted):
    for i in range(3):
        dr = di = None
        for j in range(3):
            ur, ui = link(i, j)
            vr, vi = shifted[j], shifted[3 + j]
            tr, ti = ur * vr - ui * vi, ui * vr + ur * vi
            dr, di = (tr, ti) if dr is None else (dr + tr, di + ti)
        yield i, dr, di


def complex_parts(full):
    top, bottom = full[:128], full[128:]
    return top[:, :128] + bottom[:, 128:], top[:, 128:] - bottom[:, :128]


def factor_kernel(
    mom_hbm, dir_hbm, u, v_ref, wide, vt, lt, ub, lf0_ref, lf1_ref, uf_ref, asked_ref,
    mom, dirs, sems, vo, vl, us, ut,
):
    copies = [
        pltpu.make_async_copy(mom_hbm, mom, sems.at[0]),
        pltpu.make_async_copy(dir_hbm, dirs, sems.at[1]),
    ]
    for copy in copies:
        copy.start()
    index = lax.axis_index("xyz")
    gx, gy, gz, core = index // 16, 3 - (index // 4) % 4, index % 4, index % 2

    row, column = iota((256, NVEC), 0), iota((256, NVEC), 1)
    whose = jnp.where(row < 128, 1 - core, core)
    order = (column == 4 * ((row >> 2) & 31) + 2 * whose + (row & 1)).astype(BF16)
    plain = (iota((NVEC, NVEC), 0) == iota((NVEC, NVEC), 1)).astype(BF16)
    both = jnp.concatenate([plain, order], axis=0)
    faces = []
    for rc in range(6):
        turned = lax.dot_general(both, v_ref[rc], NT, preferred_element_type=F32)
        for k in range(4):
            vt[rc, k] = turned[:128, k * 128 : k * 128 + 128]
        vo[rc] = turned[128:]
        faces.append([rows.astype(BF16) for rows in layers(wide, rc, SIDE - 1)])
    for d in range(3):
        for r in range(2):
            last = jnp.concatenate([faces[r * 3 + c][d] for c in range(3)], axis=0)
            vl[d * 2 + r] = lax.dot_general(order, last, NT, preferred_element_type=F32)
    for copy in copies:
        copy.wait()
    for slot in range(3):
        asked_ref[slot] = jnp.full((8, NVEC), dirs[slot], jnp.int32)

    def phase(site):
        lx, ly, lz = site >> 6, (site >> 3) & 7, site & 7
        second = ((iota(site.shape, 0) >> 1) & 1) == 1
        m = [jnp.where(second, mom[1, axis], mom[0, axis]) for axis in range(3)]
        k = (m[0] * (gx * 8 + lx) + m[1] * (gy * 8 + ly) + m[2] * (gz * 8 + lz)) & 31
        angle = k.astype(F32) * (2.0 * math.pi / 32)
        return jnp.cos(angle)[None], jnp.sin(angle)[None]

    def rotate(re, im, turn, width):
        cosine, sine = turn
        re, im = re.reshape(-1, 8, width), im.reshape(-1, 8, width)
        left = (cosine * re - sine * im).reshape(-1, width).astype(BF16)
        return left, (sine * re + cosine * im).reshape(-1, width).astype(BF16)

    site = iota((8, SITES), 1)
    turn = phase(site)
    for block in range(16):
        rows = pl.ds(block * 16, 16)
        for c in range(3):
            left = rotate(vo[c, rows, :], vo[3 + c, rows, :], turn, SITES)
            for ri in range(2):
                out = pl.ds((block // 8) * 256 + ri * 128 + (block % 8) * 16, 16)
                lt[out, pl.ds(c * SITES, SITES)] = left[ri]
    for d in range(3):
        turn = phase(face_site(iota((8, 3 * FACE), 1) & 63, d))
        left = rotate(vl[d * 2], vl[d * 2 + 1], turn, 3 * FACE)
        for ri in range(2):
            lf0_ref[d, pl.ds(ri * 128, 128), :] = left[ri][:128]
            lf1_ref[d, pl.ds(ri * 128, 128), :] = left[ri][128:]

    inner = [(n < SIDE - 1).astype(F32) for n in (site >> 6, (site >> 3) & 7, site & 7)]
    us[pl.ds(54, 74), :] = jnp.zeros((74, SITES), F32)
    for d in range(3):
        for ij in range(9):
            pair = u[d * 9 + ij].astype(F32)
            us[pl.ds((d * 9 + ij) * 2, 2), :] = pair
            for r in range(2):
                ub[d * 18 + ij * 2 + r] = pair[r : r + 1] * inner[d]
    for k in range(4):
        ut[0, pl.ds(k * 128, 128), :] = us[:, k * 128 : k * 128 + 128].T
    for d, rows in enumerate(layers(ut, 0, SIDE - 1)):
        uf_ref[d] = rows


def interior_kernel(vt, lt, ub, uf_ref, part0_ref, part1_ref, wide_ref, rt):
    upper = iota((16, 128), 1) >= 64

    def products(d, h):
        for block in range(8):
            rows = pl.ds(block * 16, 16)
            for k in (2 * h, 2 * h + 1):
                lanes = pl.ds(k * 128, 128)
                shifted = []
                for rc in range(6):
                    here = pltpu.roll(vt[rc, k, rows, :], (64, 120, 127)[d], 1)
                    if d == 0 and k < 3:
                        after = pltpu.roll(vt[rc, k + 1, rows, :], 64, 1)
                        here = jnp.where(upper, after, here)
                    shifted.append(here.reshape(2, 8, 128))

                def link(i, j):
                    q = d * 18 + i * 6 + j * 2
                    return ub[q, :, lanes][None], ub[q + 1, :, lanes][None]

                for i, dr, di in link_product(link, shifted):
                    lanes_out = pl.ds(i * SITES + k * 128, 128)
                    rt[d, rows, lanes_out] = dr.reshape(16, 128).astype(BF16)
                    rt[d, pl.ds(128 + block * 16, 16), lanes_out] = di.reshape(16, 128).astype(BF16)
                yield

    def contraction(sums, d, h):
        for c in range(3):
            lanes, stage = pl.ds((c * 2 + h) * 256, 256), (c + h) % 2
            for m in range(2):
                pltpu.matmul_push_rhs(rt[d, :, lanes], stage, m, transpose=True)
            for n in range(4):
                for m in range(2):
                    rows = lt[pl.ds(m * 256 + n * 64, 64), lanes]
                    pltpu.matmul_acc_lhs(sums[m][d][n], rows, stage if n == 0 else None)
                yield

    def finish(sums, d):
        for m, out_ref in enumerate((part0_ref, part1_ref)):
            for n in range(2):
                rows = pl.ds(n * 64, 64)
                top, bottom = pltpu.matmul_pop(sums[m][d][n]), pltpu.matmul_pop(sums[m][d][n + 2])
                out_ref[d * 2, rows, :] = top[:, :128] + bottom[:, 128:]
                out_ref[d * 2 + 1, rows, :] = top[:, 128:] - bottom[:, :128]

    def widen(d, h):
        for n in range(d * 18 + h * 9, d * 18 + h * 9 + 9):
            wide_ref[n] = jnp.broadcast_to(uf_ref[d, :, n : n + 1], (FACE, NVEC))

    def steps(sums):
        work = iter(())
        for d in range(3):
            for h in range(2):
                widen(d, h)
                for n, _ in enumerate(products(d, h)):
                    if n % 4 != 3:
                        next(work, None)
                for _ in work:
                    pass
                if h == 0 and d > 0:
                    finish(sums, d - 1)
                work = contraction(sums, d, h)
        for _ in work:
            pass
        finish(sums, 2)

    pl.run_scoped(steps, [[[pltpu.ACC(m)((64, 256), F32)] * 4 for _ in range(3)] for m in range(2)])


def boundary_half(part_ref, lf_ref, right, chunk):
    low = iota((16, 8, NVEC), 1) < 4
    for d in range(3):
        term = jnp.dot(lf_ref[d], right(d), preferred_element_type=F32)
        re, im = complex_parts(term)
        re = (part_ref[d * 2] + re).reshape(16, 8, NVEC)
        im = (part_ref[d * 2 + 1] + im).reshape(16, 8, NVEC)
        even = jnp.where(low, re, pltpu.roll(im, 4, 1))
        odd = jnp.where(low, pltpu.roll(re, 4, 1), im)
        pairs = jnp.stack([even, odd], axis=1).reshape(32, 8, NVEC)
        chunk[:, pl.ds(d * 8, 8), :] = pairs


def send_kernel(part_ref, lf_ref, uf_ref, x_ref, y_ref, z_ref, send_ref, right_ref, chunk):
    for d, layer_ref in enumerate((x_ref, y_ref, z_ref)):

        def link(i, j):
            q = d * 18 + i * 6 + j * 2
            return uf_ref[q, rows, :], uf_ref[q + 1, rows, :]

        for block in range(4):
            rows = pl.ds(block * 16, 16)
            layer = [layer_ref[rc, rows, :].astype(F32) for rc in range(6)]
            for i, dr, di in link_product(link, layer):
                out = pl.ds(i * FACE + block * 16, 16)
                right_ref[d, out, pl.ds(0, NVEC)] = dr.astype(BF16)
                right_ref[d, out, pl.ds(NVEC, NVEC)] = di.astype(BF16)
    boundary_half(part_ref, lf_ref, lambda d: right_ref[d], chunk)
    send_ref[...] = chunk[...].reshape(768, NVEC).astype(BF16)


def keep_kernel(part_ref, lf_ref, right_ref, keep_ref, chunk):
    boundary_half(part_ref, lf_ref, lambda d: right_ref[d], chunk)
    keep_ref[...] = chunk[...].reshape(768, NVEC)


def final_kernel(scale, asked_ref, got_ref, out_ref):
    rows = jnp.sum(got_ref[...].astype(F32), axis=0) * scale
    for slot in range(3):
        chosen = jnp.where(asked_ref[slot] == 1, rows[8:16], rows[0:8])
        chosen = jnp.where(asked_ref[slot] == 2, rows[16:24], chosen)
        for o in range(2):
            for p in range(2):
                t = o * 4 + p * 2
                out_ref[o, slot, p] = chosen[t : t + 2]


def shape(dims, dtype):
    return jax.ShapeDtypeStruct(dims, dtype)


def per_device(vectors, links, momenta, directions):
    params = pltpu.CompilerParams(vmem_limit_bytes=16 * 1024 * 1024)
    field = vectors.reshape(6, SITES, NVEC)
    rows = links.transpose(0, 2, 3, 1, 4).reshape(27, 2, SITES)
    face = shape((6, FACE, NVEC), BF16)
    held, wide, *first = pl.pallas_call(
        layer_kernel,
        out_shape=[shape((6, SITES, NVEC), BF16), shape((6, SITES, NVEC), F32)] + [face] * 3,
        in_specs=[VMEM],
        out_specs=[VMEM] * 5,
        input_output_aliases={0: 0},
        compiler_params=params,
    )(field)
    step_x = [(i, (i - 16) % 64) for i in range(64)]
    step_y = [(i, (i & ~12) | ((i + 4) & 12)) for i in range(64)]
    step_z = [(i, (i & ~3) | ((i - 1) & 3)) for i in range(64)]
    arrived = [lax.ppermute(a, "xyz", s) for a, s in zip(first, (step_x, step_y, step_z))]
    part = shape((6, NVEC, NVEC), F32)
    left = shape((3, 256, 3 * FACE), BF16)
    turned, left_all, spread, left0, left1, link_face, asked = pl.pallas_call(
        factor_kernel,
        out_shape=[
            shape((6, 4, NVEC, 128), F32),
            shape((512, 3 * SITES), BF16),
            shape((54, 8, SITES), F32),
            *[left, left],
            shape((3, FACE, NVEC), F32),
            shape((3, 8, NVEC), jnp.int32),
        ],
        in_specs=[HBM] * 2 + [VMEM] * 3,
        out_specs=[VMEM] * 7,
        scratch_shapes=[
            pltpu.SMEM((2, 3), jnp.int32),
            pltpu.SMEM((3,), jnp.int32),
            pltpu.SemaphoreType.DMA((2,)),
            pltpu.VMEM((6, 256, SITES), F32),
            pltpu.VMEM((6, 256, 3 * FACE), F32),
            pltpu.VMEM((128, SITES), F32),
            pltpu.VMEM((1, SITES, 128), F32),
        ],
        compiler_params=params,
    )(
        pltpu.with_memory_space_constraint(momenta, pltpu.HBM),
        pltpu.with_memory_space_constraint(directions, pltpu.HBM),
        *[rows, held, wide],
    )
    part0, part1, link_wide = pl.pallas_call(
        interior_kernel,
        out_shape=[part, part, shape((54, FACE, NVEC), F32)],
        in_specs=[VMEM] * 4,
        out_specs=[VMEM] * 3,
        scratch_shapes=[pltpu.VMEM((3, 256, 3 * SITES), BF16)],
        compiler_params=params,
        cost_estimate=pl.CostEstimate(
            flops=2_000_000_000, bytes_accessed=4_000_000, transcendentals=0
        ),
    )(turned, left_all, spread, link_face)
    send, right = pl.pallas_call(
        send_kernel,
        out_shape=[shape((768, NVEC), BF16), shape((3, 3 * FACE, 256), BF16)],
        in_specs=[VMEM] * 6,
        out_specs=[VMEM] * 2,
        scratch_shapes=[pltpu.VMEM((32, 24, NVEC), F32)],
        compiler_params=params,
    )(part0, left0, link_wide, *arrived)
    other = lax.ppermute(send, "xyz", [(i, i ^ 1) for i in range(64)])
    keep = pl.pallas_call(
        keep_kernel,
        out_shape=shape((768, NVEC), F32),
        in_specs=[VMEM] * 3,
        out_specs=VMEM,
        scratch_shapes=[pltpu.VMEM((32, 24, NVEC), F32)],
        compiler_params=params,
    )(part1, left1, right)
    chip = (keep + other.astype(F32)).astype(BF16).reshape(32, 24, NVEC)
    groups = [[2 * c + core for c in range(32)] for core in range(2)]
    got = lax.all_to_all(chip, "xyz", 0, 0, axis_index_groups=groups, tiled=True)
    return pl.pallas_call(
        functools.partial(final_kernel, 1.0 / math.sqrt(3.0 * SITES * 64)),
        out_shape=shape((2, 3, 2, 2, NVEC), F32),
        in_specs=[VMEM] * 2,
        out_specs=VMEM,
        compiler_params=params,
    )(asked, got)


def solution(mesh):
    in_specs = (P("ta", None, "xyz", None), P("ta", None, None, None, "xyz"), P(), P())
    out_specs = P("ta", None, None, "xyz", None)
    return jax.shard_map(
        per_device, mesh=mesh, in_specs=in_specs, out_specs=out_specs, check_vma=False
    )
```

```python
import functools
import math

import jax
import jax.numpy as jnp
from jax import lax
from jax.experimental import pallas as pl
from jax.experimental.pallas import tpu as pltpu
from jax.sharding import PartitionSpec as P

SIDE = 8
SITES = 512
FACE = 64
NVEC = 128
F32 = jnp.float32
BF16 = jnp.bfloat16
VMEM = pl.BlockSpec(memory_space=pltpu.VMEM)
HBM = pl.BlockSpec(memory_space=pltpu.HBM)
NT = (((1,), (1,)), ((), ()))


def iota(dims, axis):
    return lax.broadcasted_iota(jnp.int32, dims, axis)


def face_site(face, direction):
    hi, lo = face >> 3, face & 7
    return ((SIDE - 1) * 64 + face, hi * 64 + (SIDE - 1) * 8 + lo, face * 8 + SIDE - 1)[direction]


PLACES = (0, 4, 1, 5, 2, 6, 3, 7)


def layers(ref, index, layer):
    yield ref[index, pl.ds(layer * 64, 64), :]
    yield jnp.concatenate([ref[index, pl.ds(n * 64 + layer * 8, 8), :] for n in range(8)], axis=0)
    yield ref[index, pl.ds(layer, 64, stride=8), :]


def layer_kernel(v_ref, held_ref, wide, x_ref, y_ref, z_ref):
    for rc in range(6):
        wide[rc] = v_ref[rc].astype(F32)
        for out_ref, rows in zip((x_ref, y_ref, z_ref), layers(wide, rc, 0)):
            out_ref[rc] = rows.astype(BF16)


def link_product(link, shifted):
    for i in range(3):
        dr = di = None
        for j in range(3):
            ur, ui = link(i, j)
            vr, vi = shifted[j], shifted[3 + j]
            tr, ti = ur * vr - ui * vi, ui * vr + ur * vi
            dr, di = (tr, ti) if dr is None else (dr + tr, di + ti)
        yield i, dr, di


def link_product_of_three(link, shifted):
    both = [shifted[j] + shifted[3 + j] for j in range(3)]
    for i in range(3):
        sums = None
        for j in range(3):
            real, less, more = link(i, j)
            terms = (real * both[j], less * shifted[j], more * shifted[3 + j])
            sums = terms if sums is None else [a + b for a, b in zip(sums, terms)]
        yield i, sums[0] - sums[2], sums[0] + sums[1]


def complex_parts(full):
    top, bottom = full[:128], full[128:]
    return top[:, :128] + bottom[:, 128:], top[:, 128:] - bottom[:, :128]


def factor_kernel(
    mom_hbm, dir_hbm, u, v_ref, wide, vt, lt, ub, lf0_ref, lf1_ref, uf_ref, asked_ref,
    mom, dirs, sems, vo, vl, us, ut,
):
    copies = [
        pltpu.make_async_copy(mom_hbm, mom, sems.at[0]),
        pltpu.make_async_copy(dir_hbm, dirs, sems.at[1]),
    ]
    for copy in copies:
        copy.start()
    index = lax.axis_index("xyz")
    gx, gy, gz, core = index // 16, 3 - (index // 4) % 4, index % 4, index % 2

    row, column = iota((256, NVEC), 0), iota((256, NVEC), 1)
    whose = jnp.where(row < 128, 1 - core, core)
    order = (column == 4 * ((row >> 2) & 31) + 2 * whose + (row & 1)).astype(BF16)
    plain = (iota((NVEC, NVEC), 0) == iota((NVEC, NVEC), 1)).astype(BF16)
    both = jnp.concatenate([plain, order], axis=0)
    faces = []
    for rc in range(6):
        field = jnp.concatenate([v_ref[rc, pl.ds(n * 64, 64), :] for n in PLACES], axis=0)
        turned = lax.dot_general(both, field, NT, preferred_element_type=F32)
        for k in range(4):
            vt[rc, k] = turned[:128, k * 128 : k * 128 + 128]
        vo[rc] = turned[128:]
        faces.append([rows.astype(BF16) for rows in layers(wide, rc, SIDE - 1)])
    for d in range(3):
        for r in range(2):
            last = jnp.concatenate([faces[r * 3 + c][d] for c in range(3)], axis=0)
            vl[d * 2 + r] = lax.dot_general(order, last, NT, preferred_element_type=F32)
    for copy in copies:
        copy.wait()
    for slot in range(3):
        asked_ref[slot] = jnp.full((8, NVEC), dirs[slot], jnp.int32)

    def phase(site):
        lx, ly, lz = site >> 6, (site >> 3) & 7, site & 7
        second = ((iota(site.shape, 0) >> 1) & 1) == 1
        m = [jnp.where(second, mom[1, axis], mom[0, axis]) for axis in range(3)]
        k = (m[0] * (gx * 8 + lx) + m[1] * (gy * 8 + ly) + m[2] * (gz * 8 + lz)) & 31
        angle = k.astype(F32) * (2.0 * math.pi / 32)
        return jnp.cos(angle)[None], jnp.sin(angle)[None]

    def rotate(re, im, turn, width):
        cosine, sine = turn
        re, im = re.reshape(-1, 8, width), im.reshape(-1, 8, width)
        left = (cosine * re - sine * im).reshape(-1, width).astype(BF16)
        return left, (sine * re + cosine * im).reshape(-1, width).astype(BF16)

    lane = iota((8, SITES), 1)
    site = (((lane >> 7) + 4 * ((lane >> 6) & 1)) << 6) + (lane & 63)
    turn = phase(site)
    for block in range(16):
        rows = pl.ds(block * 16, 16)
        for c in range(3):
            left = rotate(vo[c, rows, :], vo[3 + c, rows, :], turn, SITES)
            for ri in range(2):
                out = pl.ds((block // 8) * 256 + ri * 128 + (block % 8) * 16, 16)
                lt[out, pl.ds(c * SITES, SITES)] = left[ri]
    for d in range(3):
        turn = phase(face_site(iota((8, 3 * FACE), 1) & 63, d))
        left = rotate(vl[d * 2], vl[d * 2 + 1], turn, 3 * FACE)
        for ri in range(2):
            lf0_ref[d, pl.ds(ri * 128, 128), :] = left[ri][:128]
            lf1_ref[d, pl.ds(ri * 128, 128), :] = left[ri][128:]

    inner = [(n < SIDE - 1).astype(F32) for n in (site >> 6, (site >> 3) & 7, site & 7)]
    us[pl.ds(54, 74), :] = jnp.zeros((74, SITES), F32)
    for n in range(27):
        us[pl.ds(n * 2, 2), :] = u[n].astype(F32)
    placed = jnp.concatenate([us[pl.ds(0, 56), n * 64 : n * 64 + 64] for n in PLACES], axis=1)
    for d in range(3):
        for ij in range(9):
            n = (d * 9 + ij) * 2
            real, imag = placed[n : n + 1] * inner[d], placed[n + 1 : n + 2] * inner[d]
            for n, row in enumerate((real, imag - real, imag + real)):
                ub[d * 27 + ij * 3 + n] = row
    for k in range(4):
        ut[0, pl.ds(k * 128, 128), :] = us[:, k * 128 : k * 128 + 128].T
    for d, rows in enumerate(layers(ut, 0, SIDE - 1)):
        uf_ref[d] = rows


def interior_kernel(vt, lt, ub, uf_ref, part0_ref, part1_ref, wide_ref, rt):
    def products(d, h):
        for block in range(8):
            rows = pl.ds(block * 16, 16)
            for k in (2 * h, 2 * h + 1):
                lanes = pl.ds(k * 128, 128)
                shifted = []
                for rc in range(6):
                    if d == 0 and k < 3:
                        here = vt[rc, k + 1, rows, :]
                    elif d == 0:
                        here = pltpu.roll(vt[rc, 0, rows, :], 64, 1)
                    else:
                        here = pltpu.roll(vt[rc, k, rows, :], (0, 120, 127)[d], 1)
                    shifted.append(here.reshape(2, 8, 128))

                def link(i, j):
                    q = d * 27 + i * 9 + j * 3
                    return [ub[q + n, :, lanes][None] for n in range(3)]

                for i, dr, di in link_product_of_three(link, shifted):
                    lanes_out = pl.ds(i * SITES + k * 128, 128)
                    rt[d, rows, lanes_out] = dr.reshape(16, 128).astype(BF16)
                    rt[d, pl.ds(128 + block * 16, 16), lanes_out] = di.reshape(16, 128).astype(BF16)
                yield

    def contraction(sums, d, h):
        for c in range(3):
            lanes, m, stage = pl.ds((c * 2 + h) * 256, 256), (c + h) % 2, c // 2
            pltpu.matmul_push_rhs(rt[d, :, lanes], stage, m, transpose=True)
            for n in range(8):
                rows = lt[pl.ds(n * 64, 64), lanes]
                pltpu.matmul_acc_lhs(sums[m][n], rows, stage if n == 0 else None)
                yield

    def finish(sums, d):
        rows = [pltpu.matmul_pop(sums[0][n]) + pltpu.matmul_pop(sums[1][n]) for n in range(8)]
        for half, out_ref in enumerate((part0_ref, part1_ref)):
            for n in range(2):
                place = pl.ds(n * 64, 64)
                top, bottom = rows[half * 4 + n], rows[half * 4 + n + 2]
                out_ref[d * 2, place, :] = top[:, :128] + bottom[:, 128:]
                out_ref[d * 2 + 1, place, :] = top[:, 128:] - bottom[:, :128]

    def widen(d, h):
        for n in range(d * 18 + h * 9, d * 18 + h * 9 + 9):
            wide_ref[n] = jnp.broadcast_to(uf_ref[d, :, n : n + 1], (FACE, NVEC))

    def steps(sums):
        work = iter(())
        for d in range(3):
            for h in range(2):
                widen(d, h)
                for n, _ in enumerate(products(d, h)):
                    next(work, None)
                    if n % 2:
                        next(work, None)
                for _ in work:
                    pass
                if h == 0 and d > 0:
                    finish(sums, d - 1)
                work = contraction(sums, d, h)
        for _ in work:
            pass
        finish(sums, 2)

    pl.run_scoped(steps, [[pltpu.ACC(m)((64, 256), F32)] * 8 for m in range(2)])


def boundary_half(part_ref, lf_ref, right, chunk):
    low = iota((16, 8, NVEC), 1) < 4
    for d in range(3):
        term = jnp.dot(lf_ref[d], right(d), preferred_element_type=F32)
        re, im = complex_parts(term)
        re = (part_ref[d * 2] + re).reshape(16, 8, NVEC)
        im = (part_ref[d * 2 + 1] + im).reshape(16, 8, NVEC)
        even = jnp.where(low, re, pltpu.roll(im, 4, 1))
        odd = jnp.where(low, pltpu.roll(re, 4, 1), im)
        pairs = jnp.stack([even, odd], axis=1).reshape(32, 8, NVEC)
        chunk[:, pl.ds(d * 8, 8), :] = pairs


def send_kernel(part_ref, lf_ref, uf_ref, x_ref, y_ref, z_ref, send_ref, right_ref, chunk):
    for d, layer_ref in enumerate((x_ref, y_ref, z_ref)):

        def link(i, j):
            q = d * 18 + i * 6 + j * 2
            return uf_ref[q, rows, :], uf_ref[q + 1, rows, :]

        for block in range(4):
            rows = pl.ds(block * 16, 16)
            layer = [layer_ref[rc, rows, :].astype(F32) for rc in range(6)]
            for i, dr, di in link_product(link, layer):
                out = pl.ds(i * FACE + block * 16, 16)
                right_ref[d, out, pl.ds(0, NVEC)] = dr.astype(BF16)
                right_ref[d, out, pl.ds(NVEC, NVEC)] = di.astype(BF16)
    boundary_half(part_ref, lf_ref, lambda d: right_ref[d], chunk)
    send_ref[...] = chunk[...].reshape(768, NVEC).astype(BF16)


def keep_kernel(part_ref, lf_ref, right_ref, keep_ref, chunk):
    boundary_half(part_ref, lf_ref, lambda d: right_ref[d], chunk)
    keep_ref[...] = chunk[...].reshape(768, NVEC)


def final_kernel(scale, asked_ref, got_ref, out_ref):
    rows = jnp.sum(got_ref[...].astype(F32), axis=0) * scale
    for slot in range(3):
        chosen = jnp.where(asked_ref[slot] == 1, rows[8:16], rows[0:8])
        chosen = jnp.where(asked_ref[slot] == 2, rows[16:24], chosen)
        for o in range(2):
            for p in range(2):
                t = o * 4 + p * 2
                out_ref[o, slot, p] = chosen[t : t + 2]


def shape(dims, dtype):
    return jax.ShapeDtypeStruct(dims, dtype)


def per_device(vectors, links, momenta, directions):
    params = pltpu.CompilerParams(vmem_limit_bytes=16 * 1024 * 1024)
    field = vectors.reshape(6, SITES, NVEC)
    rows = links.transpose(0, 2, 3, 1, 4).reshape(27, 2, SITES)
    face = shape((6, FACE, NVEC), BF16)
    held, wide, *first = pl.pallas_call(
        layer_kernel,
        out_shape=[shape((6, SITES, NVEC), BF16), shape((6, SITES, NVEC), F32)] + [face] * 3,
        in_specs=[VMEM],
        out_specs=[VMEM] * 5,
        input_output_aliases={0: 0},
        compiler_params=params,
    )(field)
    step_x = [(i, (i - 16) % 64) for i in range(64)]
    step_y = [(i, (i & ~12) | ((i + 4) & 12)) for i in range(64)]
    step_z = [(i, (i & ~3) | ((i - 1) & 3)) for i in range(64)]
    arrived = [lax.ppermute(a, "xyz", s) for a, s in zip(first, (step_x, step_y, step_z))]
    part = shape((6, NVEC, NVEC), F32)
    left = shape((3, 256, 3 * FACE), BF16)
    turned, left_all, spread, left0, left1, link_face, asked = pl.pallas_call(
        factor_kernel,
        out_shape=[
            shape((6, 4, NVEC, 128), F32),
            shape((512, 3 * SITES), BF16),
            shape((81, 8, SITES), F32),
            *[left, left],
            shape((3, FACE, NVEC), F32),
            shape((3, 8, NVEC), jnp.int32),
        ],
        in_specs=[HBM] * 2 + [VMEM] * 3,
        out_specs=[VMEM] * 7,
        scratch_shapes=[
            pltpu.SMEM((2, 3), jnp.int32),
            pltpu.SMEM((3,), jnp.int32),
            pltpu.SemaphoreType.DMA((2,)),
            pltpu.VMEM((6, 256, SITES), F32),
            pltpu.VMEM((6, 256, 3 * FACE), F32),
            pltpu.VMEM((128, SITES), F32),
            pltpu.VMEM((1, SITES, 128), F32),
        ],
        compiler_params=params,
    )(
        pltpu.with_memory_space_constraint(momenta, pltpu.HBM),
        pltpu.with_memory_space_constraint(directions, pltpu.HBM),
        *[rows, held, wide],
    )
    part0, part1, link_wide = pl.pallas_call(
        interior_kernel,
        out_shape=[part, part, shape((54, FACE, NVEC), F32)],
        in_specs=[VMEM] * 4,
        out_specs=[VMEM] * 3,
        scratch_shapes=[pltpu.VMEM((3, 256, 3 * SITES), BF16)],
        compiler_params=params,
        cost_estimate=pl.CostEstimate(
            flops=2_000_000_000, bytes_accessed=4_000_000, transcendentals=0
        ),
    )(turned, left_all, spread, link_face)
    send, right = pl.pallas_call(
        send_kernel,
        out_shape=[shape((768, NVEC), BF16), shape((3, 3 * FACE, 256), BF16)],
        in_specs=[VMEM] * 6,
        out_specs=[VMEM] * 2,
        scratch_shapes=[pltpu.VMEM((32, 24, NVEC), F32)],
        compiler_params=params,
    )(part0, left0, link_wide, *arrived)
    other = lax.ppermute(send, "xyz", [(i, i ^ 1) for i in range(64)])
    keep = pl.pallas_call(
        keep_kernel,
        out_shape=shape((768, NVEC), F32),
        in_specs=[VMEM] * 3,
        out_specs=VMEM,
        scratch_shapes=[pltpu.VMEM((32, 24, NVEC), F32)],
        compiler_params=params,
    )(part1, left1, right)
    chip = (keep + other.astype(F32)).astype(BF16).reshape(32, 24, NVEC)
    groups = [[2 * c + core for c in range(32)] for core in range(2)]
    got = lax.all_to_all(chip, "xyz", 0, 0, axis_index_groups=groups, tiled=True)
    return pl.pallas_call(
        functools.partial(final_kernel, 1.0 / math.sqrt(3.0 * SITES * 64)),
        out_shape=shape((2, 3, 2, 2, NVEC), F32),
        in_specs=[VMEM] * 2,
        out_specs=VMEM,
        compiler_params=params,
    )(asked, got)


def solution(mesh):
    in_specs = (P("ta", None, "xyz", None), P("ta", None, None, None, "xyz"), P(), P())
    out_specs = P("ta", None, None, "xyz", None)
    return jax.shard_map(
        per_device, mesh=mesh, in_specs=in_specs, out_specs=out_specs, check_vma=False
    )
```

```python
import functools
import math

import jax
import jax.numpy as jnp
from jax import lax
from jax.experimental import pallas as pl
from jax.experimental.pallas import tpu as pltpu
from jax.sharding import PartitionSpec as P

SIDE = 8
SITES = 512
FACE = 64
NVEC = 128
F32 = jnp.float32
BF16 = jnp.bfloat16
VMEM = pl.BlockSpec(memory_space=pltpu.VMEM)
HBM = pl.BlockSpec(memory_space=pltpu.HBM)
NT = (((1,), (1,)), ((), ()))


def iota(dims, axis):
    return lax.broadcasted_iota(jnp.int32, dims, axis)


def face_site(face, direction):
    hi, lo = face >> 3, face & 7
    return ((SIDE - 1) * 64 + face, hi * 64 + (SIDE - 1) * 8 + lo, face * 8 + SIDE - 1)[direction]


PLACES = (0, 4, 1, 5, 2, 6, 3, 7)


def layers(ref, index, layer):
    yield ref[index, pl.ds(layer * 64, 64), :]
    yield jnp.concatenate([ref[index, pl.ds(n * 64 + layer * 8, 8), :] for n in range(8)], axis=0)
    yield ref[index, pl.ds(layer, 64, stride=8), :]


def layer_kernel(v_ref, held_ref, wide, x_ref, y_ref, z_ref):
    for rc in range(6):
        wide[rc] = v_ref[rc].astype(F32)
        for out_ref, rows in zip((x_ref, y_ref, z_ref), layers(wide, rc, 0)):
            out_ref[rc] = rows.astype(BF16)


def link_product(link, shifted):
    for i in range(3):
        dr = di = None
        for j in range(3):
            ur, ui = link(i, j)
            vr, vi = shifted[j], shifted[3 + j]
            tr, ti = ur * vr - ui * vi, ui * vr + ur * vi
            dr, di = (tr, ti) if dr is None else (dr + tr, di + ti)
        yield i, dr, di


def link_product_of_three(link, shifted):
    both = [shifted[j] + shifted[3 + j] for j in range(3)]
    for i in range(3):
        sums = None
        for j in range(3):
            real, less, more = link(i, j)
            terms = (real * both[j], less * shifted[j], more * shifted[3 + j])
            sums = terms if sums is None else [a + b for a, b in zip(sums, terms)]
        yield i, sums[0] - sums[2], sums[0] + sums[1]


def complex_parts(full):
    top, bottom = full[:128], full[128:]
    return top[:, :128] + bottom[:, 128:], top[:, 128:] - bottom[:, :128]


def factor_kernel(
    mom_hbm, dir_hbm, u, v_ref, wide, vt, lt, ub, lf0_ref, lf1_ref, uf_ref, asked_ref,
    mom, dirs, sems, vo, vl, us, ut,
):
    copies = [
        pltpu.make_async_copy(mom_hbm, mom, sems.at[0]),
        pltpu.make_async_copy(dir_hbm, dirs, sems.at[1]),
    ]
    for copy in copies:
        copy.start()
    index = lax.axis_index("xyz")
    gx, gy, gz, core = index // 16, 3 - (index // 4) % 4, index % 4, index % 2

    row, column = iota((256, NVEC), 0), iota((256, NVEC), 1)
    whose = jnp.where(row < 128, 1 - core, core)
    order = (column == 4 * ((row >> 2) & 31) + 2 * whose + (row & 1)).astype(BF16)
    plain = (iota((NVEC, NVEC), 0) == iota((NVEC, NVEC), 1)).astype(BF16)
    both = jnp.concatenate([plain, order], axis=0)
    faces = []
    for rc in range(6):
        field = jnp.concatenate([v_ref[rc, pl.ds(n * 64, 64), :] for n in PLACES], axis=0)
        turned = lax.dot_general(both, field, NT, preferred_element_type=F32)
        for k in range(4):
            vt[rc, k] = turned[:128, k * 128 : k * 128 + 128]
        vo[rc] = turned[128:]
        faces.append([rows.astype(BF16) for rows in layers(wide, rc, SIDE - 1)])
    for d in range(3):
        for r in range(2):
            last = jnp.concatenate([faces[r * 3 + c][d] for c in range(3)], axis=0)
            vl[d * 2 + r] = lax.dot_general(order, last, NT, preferred_element_type=F32)
    for copy in copies:
        copy.wait()
    for slot in range(3):
        asked_ref[slot] = jnp.full((8, NVEC), dirs[slot], jnp.int32)

    def phase(site):
        lx, ly, lz = site >> 6, (site >> 3) & 7, site & 7
        second = ((iota(site.shape, 0) >> 1) & 1) == 1
        m = [jnp.where(second, mom[1, axis], mom[0, axis]) for axis in range(3)]
        k = (m[0] * (gx * 8 + lx) + m[1] * (gy * 8 + ly) + m[2] * (gz * 8 + lz)) & 31
        angle = k.astype(F32) * (2.0 * math.pi / 32)
        return jnp.cos(angle)[None], jnp.sin(angle)[None]

    def rotate(re, im, turn, width):
        cosine, sine = turn
        re, im = re.reshape(-1, 8, width), im.reshape(-1, 8, width)
        left = (cosine * re - sine * im).reshape(-1, width).astype(BF16)
        return left, (sine * re + cosine * im).reshape(-1, width).astype(BF16)

    lane = iota((8, SITES), 1)
    site = (((lane >> 7) + 4 * ((lane >> 6) & 1)) << 6) + (lane & 63)
    turn = phase(site)
    for block in range(16):
        rows = pl.ds(block * 16, 16)
        for c in range(3):
            left = rotate(vo[c, rows, :], vo[3 + c, rows, :], turn, SITES)
            for ri in range(2):
                out = pl.ds((block // 8) * 256 + ri * 128 + (block % 8) * 16, 16)
                lt[out, pl.ds(c * SITES, SITES)] = left[ri]
    for d in range(3):
        turn = phase(face_site(iota((8, 3 * FACE), 1) & 63, d))
        left = rotate(vl[d * 2], vl[d * 2 + 1], turn, 3 * FACE)
        for ri in range(2):
            lf0_ref[d, pl.ds(ri * 128, 128), :] = left[ri][:128]
            lf1_ref[d, pl.ds(ri * 128, 128), :] = left[ri][128:]

    inner = [(n < SIDE - 1).astype(F32) for n in (site >> 6, (site >> 3) & 7, site & 7)]
    us[pl.ds(54, 74), :] = jnp.zeros((74, SITES), F32)
    for n in range(27):
        us[pl.ds(n * 2, 2), :] = u[n].astype(F32)
    placed = jnp.concatenate([us[pl.ds(0, 56), n * 64 : n * 64 + 64] for n in PLACES], axis=1)
    for d in range(3):
        for ij in range(9):
            n = (d * 9 + ij) * 2
            real, imag = placed[n : n + 1] * inner[d], placed[n + 1 : n + 2] * inner[d]
            for n, row in enumerate((real, imag - real, imag + real)):
                ub[d * 27 + ij * 3 + n] = row
    for k in range(4):
        ut[0, pl.ds(k * 128, 128), :] = us[:, k * 128 : k * 128 + 128].T
    for d, rows in enumerate(layers(ut, 0, SIDE - 1)):
        uf_ref[d] = rows


def interior_kernel(vt, lt, ub, uf_ref, part0_ref, part1_ref, wide_ref, rt):
    def products(d, h):
        for block in range(8):
            rows = pl.ds(block * 16, 16)
            for k in (2 * h, 2 * h + 1):
                lanes = pl.ds(k * 128, 128)
                shifted = []
                for rc in range(6):
                    if d == 0 and k < 3:
                        here = vt[rc, k + 1, rows, :]
                    elif d == 0:
                        here = pltpu.roll(vt[rc, 0, rows, :], 64, 1)
                    else:
                        here = pltpu.roll(vt[rc, k, rows, :], (0, 120, 127)[d], 1)
                    shifted.append(here.reshape(2, 8, 128))

                def link(i, j):
                    q = d * 27 + i * 9 + j * 3
                    return [ub[q + n, :, lanes][None] for n in range(3)]

                for i, dr, di in link_product_of_three(link, shifted):
                    lanes_out = pl.ds(i * SITES + k * 128, 128)
                    rt[d, rows, lanes_out] = dr.reshape(16, 128).astype(BF16)
                    rt[d, pl.ds(128 + block * 16, 16), lanes_out] = di.reshape(16, 128).astype(BF16)
                yield

    def contraction(sums, d, h):
        for c in range(3):
            lanes, m, stage = pl.ds((c * 2 + h) * 256, 256), (c + h) % 2, c // 2
            pltpu.matmul_push_rhs(rt[d, :, lanes], stage, m, transpose=True)
            for n in range(8):
                rows = lt[pl.ds(n * 64, 64), lanes]
                pltpu.matmul_acc_lhs(sums[m][n], rows, stage if n == 0 else None)
                yield

    def finish(sums, d):
        rows = [pltpu.matmul_pop(sums[0][n]) + pltpu.matmul_pop(sums[1][n]) for n in range(8)]
        for half, out_ref in enumerate((part0_ref, part1_ref)):
            for n in range(2):
                place = pl.ds(n * 64, 64)
                top, bottom = rows[half * 4 + n], rows[half * 4 + n + 2]
                out_ref[d * 2, place, :] = top[:, :128] + bottom[:, 128:]
                out_ref[d * 2 + 1, place, :] = top[:, 128:] - bottom[:, :128]

    def widen(d, h):
        for n in range(d * 18 + h * 9, d * 18 + h * 9 + 9):
            wide_ref[n] = jnp.broadcast_to(uf_ref[d, :, n : n + 1], (FACE, NVEC))

    def steps(sums):
        work = iter(())
        for d in range(3):
            for h in range(2):
                widen(d, h)
                for n, _ in enumerate(products(d, h)):
                    next(work, None)
                    if n % 2:
                        next(work, None)
                for _ in work:
                    pass
                if h == 0 and d > 0:
                    finish(sums, d - 1)
                work = contraction(sums, d, h)
        for _ in work:
            pass
        finish(sums, 2)

    pl.run_scoped(steps, [[pltpu.ACC(m)((64, 256), F32)] * 8 for m in range(2)])


def boundary_half(d, part_ref, lf_ref, right):
    low = iota((16, 8, NVEC), 1) < 4
    re, im = complex_parts(jnp.dot(lf_ref[d], right, preferred_element_type=F32))
    re = (part_ref[d * 2] + re).reshape(16, 8, NVEC)
    im = (part_ref[d * 2 + 1] + im).reshape(16, 8, NVEC)
    even = jnp.where(low, re, pltpu.roll(im, 4, 1))
    odd = jnp.where(low, pltpu.roll(re, 4, 1), im)
    return jnp.stack([even, odd], axis=1).reshape(32, 8, NVEC)


def face_products(d, uf_ref, layer_ref, right_ref, place):
    def link(i, j):
        q = d * 18 + i * 6 + j * 2
        return uf_ref[q, rows, :], uf_ref[q + 1, rows, :]

    for block in range(4):
        rows = pl.ds(block * 16, 16)
        layer = [layer_ref[rc, rows, :].astype(F32) for rc in range(6)]
        for i, dr, di in link_product(link, layer):
            out = pl.ds(i * FACE + block * 16, 16)
            right_ref[place, out, pl.ds(0, NVEC)] = dr.astype(BF16)
            right_ref[place, out, pl.ds(NVEC, NVEC)] = di.astype(BF16)


def early_kernel(part_ref, lf_ref, uf_ref, x_ref, z_ref, early_ref, right_ref):
    for n, (d, layer_ref) in enumerate(((0, x_ref), (2, z_ref))):
        face_products(d, uf_ref, layer_ref, right_ref, n)
        early_ref[:, pl.ds(n * 8, 8), :] = boundary_half(d, part_ref, lf_ref, right_ref[n])


def send_kernel(part_ref, lf_ref, uf_ref, y_ref, early_ref, send_ref, right_ref, chunk):
    face_products(1, uf_ref, y_ref, right_ref, 0)
    chunk[:, pl.ds(0, 16), :] = early_ref[...]
    chunk[:, pl.ds(16, 8), :] = boundary_half(1, part_ref, lf_ref, right_ref[0])
    send_ref[...] = chunk[...].reshape(768, NVEC).astype(BF16)


def keep_kernel(part_ref, lf_ref, right_ref, right_y_ref, keep_ref, chunk):
    for n, d in enumerate((0, 2, 1)):
        right = right_y_ref[0] if d == 1 else right_ref[n]
        chunk[:, pl.ds(n * 8, 8), :] = boundary_half(d, part_ref, lf_ref, right)
    keep_ref[...] = chunk[...].reshape(768, NVEC)


def final_kernel(scale, asked_ref, got_ref, out_ref):
    rows = jnp.sum(got_ref[...].astype(F32), axis=0) * scale
    for slot in range(3):
        chosen = jnp.where(asked_ref[slot] == 2, rows[8:16], rows[0:8])
        chosen = jnp.where(asked_ref[slot] == 1, rows[16:24], chosen)
        for o in range(2):
            for p in range(2):
                t = o * 4 + p * 2
                out_ref[o, slot, p] = chosen[t : t + 2]


def shape(dims, dtype):
    return jax.ShapeDtypeStruct(dims, dtype)


def per_device(vectors, links, momenta, directions):
    params = pltpu.CompilerParams(vmem_limit_bytes=16 * 1024 * 1024)
    field = vectors.reshape(6, SITES, NVEC)
    rows = links.transpose(0, 2, 3, 1, 4).reshape(27, 2, SITES)
    face = shape((6, FACE, NVEC), BF16)
    held, wide, *first = pl.pallas_call(
        layer_kernel,
        out_shape=[shape((6, SITES, NVEC), BF16), shape((6, SITES, NVEC), F32)] + [face] * 3,
        in_specs=[VMEM],
        out_specs=[VMEM] * 5,
        input_output_aliases={0: 0},
        compiler_params=params,
    )(field)
    step_x = [(i, (i - 16) % 64) for i in range(64)]
    step_y = [(i, (i & ~12) | ((i + 4) & 12)) for i in range(64)]
    step_z = [(i, (i & ~3) | ((i - 1) & 3)) for i in range(64)]
    arrived = [lax.ppermute(a, "xyz", s) for a, s in zip(first, (step_x, step_y, step_z))]
    part = shape((6, NVEC, NVEC), F32)
    left = shape((3, 256, 3 * FACE), BF16)
    turned, left_all, spread, left0, left1, link_face, asked = pl.pallas_call(
        factor_kernel,
        out_shape=[
            shape((6, 4, NVEC, 128), F32),
            shape((512, 3 * SITES), BF16),
            shape((81, 8, SITES), F32),
            *[left, left],
            shape((3, FACE, NVEC), F32),
            shape((3, 8, NVEC), jnp.int32),
        ],
        in_specs=[HBM] * 2 + [VMEM] * 3,
        out_specs=[VMEM] * 7,
        scratch_shapes=[
            pltpu.SMEM((2, 3), jnp.int32),
            pltpu.SMEM((3,), jnp.int32),
            pltpu.SemaphoreType.DMA((2,)),
            pltpu.VMEM((6, 256, SITES), F32),
            pltpu.VMEM((6, 256, 3 * FACE), F32),
            pltpu.VMEM((128, SITES), F32),
            pltpu.VMEM((1, SITES, 128), F32),
        ],
        compiler_params=params,
    )(
        pltpu.with_memory_space_constraint(momenta, pltpu.HBM),
        pltpu.with_memory_space_constraint(directions, pltpu.HBM),
        *[rows, held, wide],
    )
    part0, part1, link_wide = pl.pallas_call(
        interior_kernel,
        out_shape=[part, part, shape((54, FACE, NVEC), F32)],
        in_specs=[VMEM] * 4,
        out_specs=[VMEM] * 3,
        scratch_shapes=[pltpu.VMEM((3, 256, 3 * SITES), BF16)],
        compiler_params=params,
        cost_estimate=pl.CostEstimate(
            flops=2_000_000_000, bytes_accessed=4_000_000, transcendentals=0
        ),
    )(turned, left_all, spread, link_face)
    early, right = pl.pallas_call(
        early_kernel,
        out_shape=[shape((32, 16, NVEC), F32), shape((2, 3 * FACE, 256), BF16)],
        in_specs=[VMEM] * 5,
        out_specs=[VMEM] * 2,
        compiler_params=params,
    )(part0, left0, link_wide, arrived[0], arrived[2])
    send, right_y = pl.pallas_call(
        send_kernel,
        out_shape=[shape((768, NVEC), BF16), shape((1, 3 * FACE, 256), BF16)],
        in_specs=[VMEM] * 5,
        out_specs=[VMEM] * 2,
        scratch_shapes=[pltpu.VMEM((32, 24, NVEC), F32)],
        compiler_params=params,
    )(part0, left0, link_wide, arrived[1], early)
    other = lax.ppermute(send, "xyz", [(i, i ^ 1) for i in range(64)])
    keep = pl.pallas_call(
        keep_kernel,
        out_shape=shape((768, NVEC), F32),
        in_specs=[VMEM] * 4,
        out_specs=VMEM,
        scratch_shapes=[pltpu.VMEM((32, 24, NVEC), F32)],
        compiler_params=params,
    )(part1, left1, right, right_y)
    chip = (keep + other.astype(F32)).astype(BF16).reshape(32, 24, NVEC)
    groups = [[2 * c + core for c in range(32)] for core in range(2)]
    got = lax.all_to_all(chip, "xyz", 0, 0, axis_index_groups=groups, tiled=True)
    return pl.pallas_call(
        functools.partial(final_kernel, 1.0 / math.sqrt(3.0 * SITES * 64)),
        out_shape=shape((2, 3, 2, 2, NVEC), F32),
        in_specs=[VMEM] * 2,
        out_specs=VMEM,
        compiler_params=params,
    )(asked, got)


def solution(mesh):
    in_specs = (P("ta", None, "xyz", None), P("ta", None, None, None, "xyz"), P(), P())
    out_specs = P("ta", None, None, "xyz", None)
    return jax.shard_map(
        per_device, mesh=mesh, in_specs=in_specs, out_specs=out_specs, check_vma=False
    )
```

```python
import functools
import math

import jax
import jax.numpy as jnp
from jax import lax
from jax.experimental import pallas as pl
from jax.experimental.pallas import tpu as pltpu
from jax.sharding import PartitionSpec as P

SIDE = 8
SITES = 512
FACE = 64
NVEC = 128
F32 = jnp.float32
BF16 = jnp.bfloat16
VMEM = pl.BlockSpec(memory_space=pltpu.VMEM)
HBM = pl.BlockSpec(memory_space=pltpu.HBM)
NT = (((1,), (1,)), ((), ()))


def iota(dims, axis):
    return lax.broadcasted_iota(jnp.int32, dims, axis)


def face_site(face, direction):
    hi, lo = face >> 3, face & 7
    return ((SIDE - 1) * 64 + face, hi * 64 + (SIDE - 1) * 8 + lo, face * 8 + SIDE - 1)[direction]


PLACES = (0, 4, 1, 5, 2, 6, 3, 7)


def layers(ref, index, layer):
    yield ref[index, pl.ds(layer * 64, 64), :]
    yield jnp.concatenate([ref[index, pl.ds(n * 64 + layer * 8, 8), :] for n in range(8)], axis=0)
    yield ref[index, pl.ds(layer, 64, stride=8), :]


def layer_kernel(v_ref, held_ref, wide, x_ref, y_ref, z_ref):
    for rc in range(6):
        wide[rc] = v_ref[rc].astype(F32)
        for out_ref, rows in zip((x_ref, y_ref, z_ref), layers(wide, rc, 0)):
            out_ref[rc] = rows.astype(BF16)


def link_product(link, shifted):
    for i in range(3):
        dr = di = None
        for j in range(3):
            ur, ui = link(i, j)
            vr, vi = shifted[j], shifted[3 + j]
            tr, ti = ur * vr - ui * vi, ui * vr + ur * vi
            dr, di = (tr, ti) if dr is None else (dr + tr, di + ti)
        yield i, dr, di


def link_product_of_three(link, shifted):
    both = [shifted[j] + shifted[3 + j] for j in range(3)]
    for i in range(3):
        sums = None
        for j in range(3):
            real, less, more = link(i, j)
            terms = (real * both[j], less * shifted[j], more * shifted[3 + j])
            sums = terms if sums is None else [a + b for a, b in zip(sums, terms)]
        yield i, sums[0] - sums[2], sums[0] + sums[1]


def complex_parts(full):
    top, bottom = full[:128], full[128:]
    return top[:, :128] + bottom[:, 128:], top[:, 128:] - bottom[:, :128]


def factor_kernel(
    mom_hbm, dir_hbm, u, v_ref, wide, vt, lt, ub, lf0_ref, lf1_ref, uf_ref, asked_ref,
    mom, dirs, sems, vo, vl, us, ut,
):
    copies = [
        pltpu.make_async_copy(mom_hbm, mom, sems.at[0]),
        pltpu.make_async_copy(dir_hbm, dirs, sems.at[1]),
    ]
    for copy in copies:
        copy.start()
    index = lax.axis_index("xyz")
    gx, gy, gz, core = index // 16, 3 - (index // 4) % 4, index % 4, index % 2

    row, column = iota((256, NVEC), 0), iota((256, NVEC), 1)
    whose = jnp.where(row < 128, 1 - core, core)
    order = (column == 4 * ((row >> 2) & 31) + 2 * whose + (row & 1)).astype(BF16)
    plain = (iota((NVEC, NVEC), 0) == iota((NVEC, NVEC), 1)).astype(BF16)
    both = jnp.concatenate([plain, order], axis=0)
    faces = []
    for rc in range(6):
        field = jnp.concatenate([v_ref[rc, pl.ds(n * 64, 64), :] for n in PLACES], axis=0)
        turned = lax.dot_general(both, field, NT, preferred_element_type=F32)
        for k in range(4):
            vt[rc, k] = turned[:128, k * 128 : k * 128 + 128]
        vo[rc] = turned[128:]
        faces.append([rows.astype(BF16) for rows in layers(wide, rc, SIDE - 1)])
    for d in range(3):
        for r in range(2):
            last = jnp.concatenate([faces[r * 3 + c][d] for c in range(3)], axis=0)
            vl[d * 2 + r] = lax.dot_general(order, last, NT, preferred_element_type=F32)
    for copy in copies:
        copy.wait()
    for slot in range(3):
        asked_ref[slot] = jnp.full((8, NVEC), dirs[slot], jnp.int32)

    def phase(site):
        lx, ly, lz = site >> 6, (site >> 3) & 7, site & 7
        second = ((iota(site.shape, 0) >> 1) & 1) == 1
        m = [jnp.where(second, mom[1, axis], mom[0, axis]) for axis in range(3)]
        k = (m[0] * (gx * 8 + lx) + m[1] * (gy * 8 + ly) + m[2] * (gz * 8 + lz)) & 31
        angle = k.astype(F32) * (2.0 * math.pi / 32)
        return jnp.cos(angle)[None], jnp.sin(angle)[None]

    def rotate(re, im, turn, width):
        cosine, sine = turn
        re, im = re.reshape(-1, 8, width), im.reshape(-1, 8, width)
        left = (cosine * re - sine * im).reshape(-1, width).astype(BF16)
        return left, (sine * re + cosine * im).reshape(-1, width).astype(BF16)

    lane = iota((8, SITES), 1)
    site = (((lane >> 7) + 4 * ((lane >> 6) & 1)) << 6) + (lane & 63)
    turn = phase(site)
    for block in range(16):
        rows = pl.ds(block * 16, 16)
        for c in range(3):
            left = rotate(vo[c, rows, :], vo[3 + c, rows, :], turn, SITES)
            for ri in range(2):
                out = pl.ds((block // 8) * 256 + ri * 128 + (block % 8) * 16, 16)
                lt[out, pl.ds(c * SITES, SITES)] = left[ri]
    for d in range(3):
        turn = phase(face_site(iota((8, 3 * FACE), 1) & 63, d))
        left = rotate(vl[d * 2], vl[d * 2 + 1], turn, 3 * FACE)
        for ri in range(2):
            lf0_ref[d, pl.ds(ri * 128, 128), :] = left[ri][:128]
            lf1_ref[d, pl.ds(ri * 128, 128), :] = left[ri][128:]

    inner = [(n < SIDE - 1).astype(F32) for n in (site >> 6, (site >> 3) & 7, site & 7)]
    us[pl.ds(54, 74), :] = jnp.zeros((74, SITES), F32)
    for n in range(27):
        us[pl.ds(n * 2, 2), :] = u[n].astype(F32)
    placed = jnp.concatenate([us[pl.ds(0, 56), n * 64 : n * 64 + 64] for n in PLACES], axis=1)
    for d in range(3):
        for ij in range(9):
            n = (d * 9 + ij) * 2
            real, imag = placed[n : n + 1] * inner[d], placed[n + 1 : n + 2] * inner[d]
            for n, row in enumerate((real, imag - real, imag + real)):
                ub[d * 27 + ij * 3 + n] = row
    for k in range(4):
        ut[0, pl.ds(k * 128, 128), :] = us[:, k * 128 : k * 128 + 128].T
    for d, rows in enumerate(layers(ut, 0, SIDE - 1)):
        uf_ref[d] = rows


def interior_kernel(vt, lt, ub, uf_ref, part0_ref, part1_ref, wide_ref, rt):
    def products(d, h):
        for block in range(8):
            rows = pl.ds(block * 16, 16)
            for k in (2 * h, 2 * h + 1):
                lanes = pl.ds(k * 128, 128)
                shifted = []
                for rc in range(6):
                    if d == 0 and k < 3:
                        here = vt[rc, k + 1, rows, :]
                    elif d == 0:
                        here = pltpu.roll(vt[rc, 0, rows, :], 64, 1)
                    else:
                        here = pltpu.roll(vt[rc, k, rows, :], (0, 120, 127)[d], 1)
                    shifted.append(here.reshape(2, 8, 128))

                def link(i, j):
                    q = d * 27 + i * 9 + j * 3
                    return [ub[q + n, :, lanes][None] for n in range(3)]

                for i, dr, di in link_product_of_three(link, shifted):
                    lanes_out = pl.ds(i * SITES + k * 128, 128)
                    rt[d, rows, lanes_out] = dr.reshape(16, 128).astype(BF16)
                    rt[d, pl.ds(128 + block * 16, 16), lanes_out] = di.reshape(16, 128).astype(BF16)
                yield

    def contraction(sums, d, h):
        for c in range(3):
            lanes, m, stage = pl.ds((c * 2 + h) * 256, 256), (c + h) % 2, c // 2
            pltpu.matmul_push_rhs(rt[d, :, lanes], stage, m, transpose=True)
            for n in range(8):
                rows = lt[pl.ds(n * 64, 64), lanes]
                pltpu.matmul_acc_lhs(sums[m][n], rows, stage if n == 0 else None)
                yield

    def finish(sums, d):
        rows = [pltpu.matmul_pop(sums[0][n]) + pltpu.matmul_pop(sums[1][n]) for n in range(8)]
        for half, out_ref in enumerate((part0_ref, part1_ref)):
            for n in range(2):
                place = pl.ds(n * 64, 64)
                top, bottom = rows[half * 4 + n], rows[half * 4 + n + 2]
                out_ref[d * 2, place, :] = top[:, :128] + bottom[:, 128:]
                out_ref[d * 2 + 1, place, :] = top[:, 128:] - bottom[:, :128]

    def widen(d, h):
        for n in range(d * 18 + h * 9, d * 18 + h * 9 + 9):
            wide_ref[n] = jnp.broadcast_to(uf_ref[d, :, n : n + 1], (FACE, NVEC))

    def steps(sums):
        work = iter(())
        for d in range(3):
            for h in range(2):
                widen(d, h)
                for n, _ in enumerate(products(d, h)):
                    next(work, None)
                    if n % 2:
                        next(work, None)
                for _ in work:
                    pass
                if h == 0 and d > 0:
                    finish(sums, d - 1)
                work = contraction(sums, d, h)
        for _ in work:
            pass
        finish(sums, 2)

    pl.run_scoped(steps, [[pltpu.ACC(m)((64, 256), F32)] * 8 for m in range(2)])


def boundary_half(d, part_ref, lf_ref, right):
    low = iota((16, 8, NVEC), 1) < 4
    re, im = complex_parts(jnp.dot(lf_ref[d], right, preferred_element_type=F32))
    re = (part_ref[d * 2] + re).reshape(16, 8, NVEC)
    im = (part_ref[d * 2 + 1] + im).reshape(16, 8, NVEC)
    even = jnp.where(low, re, pltpu.roll(im, 4, 1))
    odd = jnp.where(low, pltpu.roll(re, 4, 1), im)
    return jnp.stack([even, odd], axis=1).reshape(32, 8, NVEC)


def face_products(d, uf_ref, layer_ref, right_ref, place):
    def link(i, j):
        q = d * 18 + i * 6 + j * 2
        return uf_ref[q, rows, :], uf_ref[q + 1, rows, :]

    for block in range(4):
        rows = pl.ds(block * 16, 16)
        layer = [layer_ref[rc, rows, :].astype(F32) for rc in range(6)]
        for i, dr, di in link_product(link, layer):
            out = pl.ds(i * FACE + block * 16, 16)
            right_ref[place, out, pl.ds(0, NVEC)] = dr.astype(BF16)
            right_ref[place, out, pl.ds(NVEC, NVEC)] = di.astype(BF16)


def early_kernel(part_ref, lf_ref, uf_ref, x_ref, z_ref, early_ref, right_ref):
    for n, (d, layer_ref) in enumerate(((0, x_ref), (2, z_ref))):
        face_products(d, uf_ref, layer_ref, right_ref, n)
        early_ref[:, pl.ds(n * 8, 8), :] = boundary_half(d, part_ref, lf_ref, right_ref[n])


def send_kernel(x_ref, part_ref, lf_ref, uf_ref, y_ref, early_ref, send_ref, right_ref, chunk):
    face_products(1, uf_ref, y_ref, right_ref, 0)
    chunk[:, pl.ds(0, 16), :] = early_ref[...]
    chunk[:, pl.ds(16, 8), :] = boundary_half(1, part_ref, lf_ref, right_ref[0])
    send_ref[...] = chunk[...].reshape(768, NVEC).astype(BF16)


def keep_kernel(right_y_ref, part_ref, lf_ref, right_ref, keep_ref, chunk):
    for n, d in enumerate((0, 2, 1)):
        right = right_y_ref[0] if d == 1 else right_ref[n]
        chunk[:, pl.ds(n * 8, 8), :] = boundary_half(d, part_ref, lf_ref, right)
    keep_ref[...] = chunk[...].reshape(768, NVEC)


def final_kernel(scale, asked_ref, got_ref, out_ref):
    rows = jnp.sum(got_ref[...].astype(F32), axis=0) * scale
    for slot in range(3):
        chosen = jnp.where(asked_ref[slot] == 2, rows[8:16], rows[0:8])
        chosen = jnp.where(asked_ref[slot] == 1, rows[16:24], chosen)
        for o in range(2):
            for p in range(2):
                t = o * 4 + p * 2
                out_ref[o, slot, p] = chosen[t : t + 2]


def shape(dims, dtype):
    return jax.ShapeDtypeStruct(dims, dtype)


def per_device(vectors, links, momenta, directions):
    params = pltpu.CompilerParams(vmem_limit_bytes=16 * 1024 * 1024)
    field = vectors.reshape(6, SITES, NVEC)
    rows = links.transpose(0, 2, 3, 1, 4).reshape(27, 2, SITES)
    face = shape((6, FACE, NVEC), BF16)
    held, wide, *first = pl.pallas_call(
        layer_kernel,
        out_shape=[shape((6, SITES, NVEC), BF16), shape((6, SITES, NVEC), F32)] + [face] * 3,
        in_specs=[VMEM],
        out_specs=[VMEM] * 5,
        input_output_aliases={0: 0},
        compiler_params=params,
    )(field)
    step_x = [(i, (i - 16) % 64) for i in range(64)]
    step_y = [(i, (i & ~12) | ((i + 4) & 12)) for i in range(64)]
    step_z = [(i, (i & ~3) | ((i - 1) & 3)) for i in range(64)]
    arrived = [lax.ppermute(a, "xyz", s) for a, s in zip(first, (step_x, step_y, step_z))]
    part = shape((6, NVEC, NVEC), F32)
    left = shape((3, 256, 3 * FACE), BF16)
    turned, left_all, spread, left0, left1, link_face, asked = pl.pallas_call(
        factor_kernel,
        out_shape=[
            shape((6, 4, NVEC, 128), F32),
            shape((512, 3 * SITES), BF16),
            shape((81, 8, SITES), F32),
            *[left, left],
            shape((3, FACE, NVEC), F32),
            shape((3, 8, NVEC), jnp.int32),
        ],
        in_specs=[HBM] * 2 + [VMEM] * 3,
        out_specs=[VMEM] * 7,
        scratch_shapes=[
            pltpu.SMEM((2, 3), jnp.int32),
            pltpu.SMEM((3,), jnp.int32),
            pltpu.SemaphoreType.DMA((2,)),
            pltpu.VMEM((6, 256, SITES), F32),
            pltpu.VMEM((6, 256, 3 * FACE), F32),
            pltpu.VMEM((128, SITES), F32),
            pltpu.VMEM((1, SITES, 128), F32),
        ],
        compiler_params=params,
    )(
        pltpu.with_memory_space_constraint(momenta, pltpu.HBM),
        pltpu.with_memory_space_constraint(directions, pltpu.HBM),
        *[rows, held, wide],
    )
    part0, part1, link_wide = pl.pallas_call(
        interior_kernel,
        out_shape=[part, part, shape((54, FACE, NVEC), F32)],
        in_specs=[VMEM] * 4,
        out_specs=[VMEM] * 3,
        scratch_shapes=[pltpu.VMEM((3, 256, 3 * SITES), BF16)],
        compiler_params=params,
        cost_estimate=pl.CostEstimate(
            flops=2_000_000_000, bytes_accessed=4_000_000, transcendentals=0
        ),
    )(turned, left_all, spread, link_face)
    early, right = pl.pallas_call(
        early_kernel,
        out_shape=[shape((32, 16, NVEC), F32), shape((2, 3 * FACE, 256), BF16)],
        in_specs=[VMEM] * 5,
        out_specs=[VMEM] * 2,
        compiler_params=params,
    )(part0, left0, link_wide, arrived[0], arrived[2])
    send, right_y = pl.pallas_call(
        send_kernel,
        out_shape=[shape((768, NVEC), BF16), shape((1, 3 * FACE, 256), BF16)],
        in_specs=[VMEM] * 6,
        out_specs=[VMEM] * 2,
        scratch_shapes=[pltpu.VMEM((32, 24, NVEC), F32)],
        compiler_params=params,
    )(arrived[0], part0, left0, link_wide, arrived[1], early)
    other = lax.ppermute(send, "xyz", [(i, i ^ 1) for i in range(64)])
    keep = pl.pallas_call(
        keep_kernel,
        out_shape=shape((768, NVEC), F32),
        in_specs=[VMEM] * 4,
        out_specs=VMEM,
        scratch_shapes=[pltpu.VMEM((32, 24, NVEC), F32)],
        compiler_params=params,
    )(right_y, part1, left1, right)
    chip = (keep + other.astype(F32)).astype(BF16).reshape(32, 24, NVEC)
    groups = [[2 * c + core for c in range(32)] for core in range(2)]
    got = lax.all_to_all(chip, "xyz", 0, 0, axis_index_groups=groups, tiled=True)
    return pl.pallas_call(
        functools.partial(final_kernel, 1.0 / math.sqrt(3.0 * SITES * 64)),
        out_shape=shape((2, 3, 2, 2, NVEC), F32),
        in_specs=[VMEM] * 2,
        out_specs=VMEM,
        compiler_params=params,
    )(asked, got)


def solution(mesh):
    in_specs = (P("ta", None, "xyz", None), P("ta", None, None, None, "xyz"), P(), P())
    out_specs = P("ta", None, None, "xyz", None)
    return jax.shard_map(
        per_device, mesh=mesh, in_specs=in_specs, out_specs=out_specs, check_vma=False
    )
```
